512 devices in a mesh: row: 16 (over z_lo, y), col: 32 (over z_hi, x, core).
Axes of the slice: x: 4, y: 4, z: 16 (z_hi: 4, z_lo: 4; z = z_hi * 4 + z_lo), core: 2. Of those that a mesh axis runs over, the one named last changes fastest.
Arguments:
- tokens: bfloat16 [320, 12288], P('col', 'row'), may hold values from -6 to 6
- weight_in: bfloat16 [12288, 24576], P('row', 'col'), may hold values from -0.109375 to 0.109375
- weight_out: bfloat16 [24576, 12288], P('col', 'row'), may hold values from -0.078125 to 0.078125
- mask_in: int32 [96, 192], P('row', 'col'), may hold values 0 or 1
- mask_out: int32 [192, 96], P('col', 'row'), may hold values 0 or 1
- grad_out: bfloat16 [320, 12288], P('col', 'row'), may hold values from -6 to 6
Outputs:
- output: bfloat16 [320, 12288], P('col', 'row')
- grad_tokens: bfloat16 [320, 12288], P('col', 'row')
The draws below stay inside these ranges and needn't reach their ends.
All inputs are finite; a program needn't handle non-finite values. No bound on the sum of `mask_in` or of `mask_out` on one device may be relied on, other than what follows from the above.
Results may differ from the reference program's by a relative error of at most 0.0049.
Values may be sent and summed in bfloat16 or wider, within the bound.
A program may use at most 64 MiB of HBM per device.

```python
import jax
import jax.numpy as jnp
from jax import lax

D = 12288
FF = 24576
BLOCK = 128
TOKENS = 320


def with_ends(entries, stream_key, smallest, largest):
    extent = entries.shape
    index_at = [jax.random.randint(jax.random.fold_in(stream_key, axis), (), 0, extent[axis]) for axis in range(len(extent))]
    entries = entries.at[tuple(index_at)].set(smallest)
    longest = extent.index(max(extent))
    index_at[longest] = (index_at[longest] + 1) % extent[longest]
    return entries.at[tuple(index_at)].set(largest)


def steps_of(stream_key, extent, cuts, low, top_value):
    def one(axis_at, blocks):
        steps = jax.random.uniform(jax.random.fold_in(jax.random.fold_in(stream_key, 6), axis_at), (blocks,), jnp.float32, low / len(cuts), top_value / len(cuts))
        return jnp.repeat(jnp.exp(steps), extent[axis_at] // blocks).reshape((-1,) + (1,) * (len(extent) - axis_at - 1))

    gain = one(*cuts[0])
    for cut in cuts[1:]:
        gain = gain * one(*cut)
    return gain


def noise(rng, shape, deviation, reach, pieces=(), kind=jnp.bfloat16):
    drawn = deviation * jax.random.normal(rng, shape, jnp.float32)
    if pieces:
        drawn = drawn * steps_of(rng, shape, pieces, -0.22, 0.18)
    return jnp.clip(drawn, -reach, reach).astype(kind)


def setup_inputs(seed: int = 0) -> dict:
    key_of = jax.random.split(jax.random.key(seed), 7)
    return {
        "tokens": noise(key_of[0], (TOKENS, D), 1.0, 6.0, ((0, 32), (1, 16))),
        "weight_in": noise(key_of[1], (D, FF), (D // 4) ** -0.5, 0.109375, ((0, 16), (1, 32))),
        "weight_out": noise(key_of[2], (FF, D), (FF // 4) ** -0.5, 0.078125, ((0, 32), (1, 16))),
        "mask_in": with_ends((jax.random.randint(key_of[3], (D // BLOCK, FF // BLOCK), 0, 4) < 1).astype(jnp.int32), jax.random.fold_in(key_of[3], 1), 0, 1),
        "mask_out": with_ends((jax.random.randint(key_of[4], (FF // BLOCK, D // BLOCK), 0, 4) < 1).astype(jnp.int32), jax.random.fold_in(key_of[4], 1), 0, 1),
        "grad_out": noise(key_of[5], (TOKENS, D), 1.0, 6.0, ((0, 32), (1, 16))),
    }


def expand(mask, rows):
    block = rows // mask.shape[0]
    blocks = mask.astype(jnp.bfloat16)
    return jnp.repeat(jnp.repeat(blocks, block, axis=0), block, axis=1)

def reference(tokens, weight_in, weight_out, mask_in, mask_out, grad_out):
    keep_in = expand(mask_in, weight_in.shape[0])
    keep_out = expand(mask_out, weight_out.shape[0])
    masked_in = weight_in * keep_in
    masked_out = weight_out * keep_out
    pre = jnp.dot(tokens, masked_in, preferred_element_type=jnp.float32)
    hidden = jax.nn.gelu(pre).astype(jnp.bfloat16)
    output = jnp.dot(hidden, masked_out, preferred_element_type=jnp.float32).astype(jnp.bfloat16)
    grad_hidden = lax.dot_general(grad_out, masked_out, (((1,), (1,)), ((), ())), preferred_element_type=jnp.float32)
    _, pull = jax.vjp(jax.nn.gelu, pre)
    grad_pre = pull(grad_hidden)[0].astype(jnp.bfloat16)
    grad_tokens = lax.dot_general(grad_pre, masked_in, (((1,), (1,)), ((), ())), preferred_element_type=jnp.float32).astype(jnp.bfloat16)
    return (output, grad_tokens)
```

```python
import jax
import jax.numpy as jnp
from jax import lax
from jax.experimental import pallas as pl
from jax.experimental.pallas import tpu as pltpu
from jax.sharding import PartitionSpec as P

F32, BF16 = jnp.float32, jnp.bfloat16
MESH = pl.DeviceIdType.MESH
PARTS = 2
M = 6 // PARTS
WIDE = 128 * M
ROWS = 80 * M
SHARE = -(-(20 * M) // 16) * 16
N_SEMS = 20 + 2 * PARTS * 21 + 20


def nn(a, b):
    return jnp.dot(a, b, preferred_element_type=F32)


def nt(a, b):
    return lax.dot_general(a, b, (((1,), (1,)), ((), ())), preferred_element_type=F32)


def lanes_to_rows(v):
    return jnp.concatenate(
        [v[:, 128 * j : 128 * (j + 1)] for j in range(v.shape[1] // 128)], axis=0
    )


def sigmoid_parts(v):
    u = 0.7978845608028654 * (v + 0.044715 * (v * v * v))
    return 1.0 / (1.0 + jnp.exp(jnp.minimum(-2.0 * u, 80.0)))


def kernel(
    mask_in, mask_out, tok, grad, w_in_hbm, w_out_hbm, out, gtok,
    w_in, w_out, gath, pack, unp, lhs, part_f, part_b, y_in, half_f, half_b, z_in, pre_s,
    hid, acc, sib_out, sib_in, x_out, x_in, mine, piece, zh_out, zh_in,
    w_sem, send, recv,
):
    r, c = lax.axis_index("row"), lax.axis_index("col")
    zl, y = r // 4, r % 4
    zh, x, k = c // 8, (c // 2) % 4, c % 2

    def at_y(d):
        return {"row": zl * 4 + (y + d) % 4}

    def at_zl(d):
        return {"row": ((zl + d) % 4) * 4 + y}

    def at_x(d):
        return {"col": zh * 8 + ((x + d) % 4) * 2 + k}

    def at_zh(d):
        return {"col": ((zh + d) % 4) * 8 + x * 2 + k}

    sibling = {"col": zh * 8 + x * 2 + (1 - k)}

    loads = [
        pltpu.make_async_copy(w_in_hbm, w_in, w_sem.at[0]),
        pltpu.make_async_copy(w_out_hbm, w_out, w_sem.at[1]),
    ]
    for load in loads:
        load.start()

    barrier = pltpu.get_barrier_semaphore()
    peers = [sibling]
    for d in (1, 2, 3):
        peers += [at_zh(d), at_x(d), at_y(d), at_zl(d)]
    for peer in peers:
        pl.semaphore_signal(barrier, inc=1, device_id=peer, device_id_type=MESH)

    started = []

    def put(src, dst, peer):
        i = len(started)
        copy = pltpu.make_async_remote_copy(
            src_ref=src, dst_ref=dst, send_sem=send.at[i], recv_sem=recv.at[i],
            device_id=peer, device_id_type=MESH,
        )
        copy.start()
        started.append(copy)
        return copy

    ins, outs = (tok, grad), (out, gtok)
    for a in (0, 1):
        v = ins[a][...].astype(F32)
        pack[a] = jnp.zeros((64, 128), F32)
        for j in range(6):
            pack[a, pl.ds(j, 10, stride=6), :] = v[:, 128 * j : 128 * (j + 1)]
        gath[a, 0, 0, 0] = pack[a].astype(BF16)
        for e in range(4):
            piece[a, e, pl.ds(56, 8), :] = jnp.zeros((8, 128), F32)
    pl.semaphore_wait(barrier, len(peers))

    zs = [
        [put(gath.at[a, 0, 0, 0], gath.at[a, 0, 0, 4 - d], at_zh(d)) for d in (1, 2, 3)]
        for a in (0, 1)
    ]
    for load in loads:
        load.wait()
    for w, mask in ((w_in, mask_in), (w_out, mask_out)):
        for i in range(6):
            rows = slice(128 * i, 128 * (i + 1))
            for j in range(6):
                cols = slice(128 * j, 128 * (j + 1))
                keep = mask[i, j].astype(F32)
                w[rows, cols] = (w[rows, cols].astype(F32) * keep).astype(BF16)
    xs, sibs = [], []
    for a in (0, 1):
        for copy in zs[a]:
            copy.wait_recv()
        xs.append(
            [put(gath.at[a, 0, 0], gath.at[a, 4 - d, 0], at_x(d)) for d in (1, 2, 3)]
        )
        sibs.append([put(gath.at[a, 0, 0], gath.at[a, 0, 1], sibling)])
    ys = {}
    for a in (0, 1):
        for d in (1, 2, 3):
            xs[a][d - 1].wait_recv()
            sibs[a].append(put(gath.at[a, 4 - d, 0], gath.at[a, 4 - d, 1], sibling))
        for copy in sibs[a]:
            copy.wait_recv()
        for s in range(32):
            d, dk, e = s // 8, (s // 4) % 2, s % 4
            unp[pl.ds(60 * s, 60), :] = gath[a, d, dk, e].astype(F32)[:60]
        for j in range(6):
            lhs[:, 128 * j : 128 * (j + 1)] = unp[pl.ds(j, 320, stride=6), :].astype(BF16)
        for n in range(PARTS):
            cols = slice(WIDE * n, WIDE * (n + 1))
            if a == 0:
                value = nn(lhs[...], w_in[:, cols])
            else:
                value = nt(lhs[...], w_out[cols, :])
            for g in range(4):
                rows = lanes_to_rows(value[80 * g : 80 * (g + 1)])
                part_f[a, n, g] = rows
                part_b[a, n, g] = rows.astype(BF16)
            ys[a, n] = [
                put(part_b.at[a, n, (y + d) % 4], y_in.at[a, n, 4 - d], at_y(d))
                for d in (1, 2, 3)
            ]

    units = [(a, n) for a in (0, 1) for n in range(PARTS)]
    zls, own = {}, {}
    for a, n in units:
        for copy in ys[a, n]:
            copy.wait_recv()
        total = part_f[a, n, y]
        for d in (1, 2, 3):
            total = total + y_in[a, n, d].astype(F32)
        if 4 * SHARE > ROWS:
            total = jnp.concatenate([total, jnp.zeros((4 * SHARE - ROWS, 128), F32)], axis=0)
        for q in range(4):
            rows = total[SHARE * q : SHARE * (q + 1)]
            half_f[a, n, q] = rows
            half_b[a, n, q] = rows.astype(BF16)
        zls[a, n] = [
            put(half_b.at[a, n, (zl + d) % 4], z_in.at[a, n, 4 - d], at_zl(d))
            for d in (1, 2, 3)
        ]
    gz, gy = {}, {}
    for a, n in units:
        for copy in zls[a, n]:
            copy.wait_recv()
        total = half_f[a, n, zl]
        for d in (1, 2, 3):
            total = total + z_in[a, n, d].astype(F32)
        if a == 0:
            pre_s[n] = total
            value = total * sigmoid_parts(total)
        else:
            v = pre_s[n]
            s = sigmoid_parts(v)
            slope = 1.5957691216057308 * (1.0 + 0.134145 * (v * v))
            value = (s + v * (s * (1.0 - s)) * slope) * total
        hid[a, n, y, zl] = value.astype(BF16)
        slot = hid.at[a, n, y, zl]
        gz[a, n] = [put(slot, slot, at_zl(d)) for d in (1, 2, 3)]
        gy[a, n] = [put(slot, slot, at_y(d)) for d in (1, 2, 3)]
    for a, n in units:
        for d in (1, 2, 3):
            gz[a, n][d - 1].wait_recv()
            slot = hid.at[a, n, y, (zl + 4 - d) % 4]
            gy[a, n] += [put(slot, slot, at_y(e)) for e in (1, 2, 3)]
    pairs = []
    for a in (0, 1):
        for n in range(PARTS):
            for copy in gy[a, n]:
                copy.wait_recv()
            cols = slice(WIDE * n, WIDE * (n + 1))
            left = jnp.concatenate(
                [
                    jnp.concatenate(
                        [
                            hid[a, n, g].reshape(4 * SHARE, 128)[80 * j : 80 * (j + 1)]
                            for j in range(M)
                        ],
                        axis=1,
                    )
                    for g in range(4)
                ],
                axis=0,
            )
            if a == 0:
                value = nn(left, w_out[cols, :])
            else:
                value = nt(left, w_in[:, cols])
            if n:
                value = value + acc[...]
            if n + 1 < PARTS:
                acc[...] = value
        pair = []
        for d in range(4):
            mine[a, d] = lanes_to_rows(value[80 * d : 80 * d + 40])
            sib_out[a, d] = lanes_to_rows(value[80 * d + 40 : 80 * d + 80])
        for d in (1, 2, 3, 0):
            pair.append(put(sib_out.at[a, d], sib_in.at[a, d], sibling))
        pairs.append(pair)
    xr = []
    for a in (0, 1):
        got = []
        for i, d in enumerate((1, 2, 3, 0)):
            pairs[a][i].wait_recv()
            total = mine[a, d] + sib_in[a, d]
            if d:
                x_out[a, d] = total.astype(BF16)
                got.append(put(x_out.at[a, d], x_in.at[a, 4 - d], at_x(d)))
            else:
                mine[a, 0] = total
        xr.append(got)
    zr = []
    for a in (0, 1):
        for copy in xr[a]:
            copy.wait_recv()
        total = mine[a, 0]
        for d in (1, 2, 3):
            total = total + x_in[a, d].astype(F32)
        mine[a, 0] = total
        for e in (1, 2, 3, 0):
            for j in range(6):
                piece[a, e, pl.ds(10 * j, 10), :] = mine[a, 0, pl.ds(40 * j + 10 * e, 10), :]
            if e:
                zh_out[a, e] = piece[a, e].astype(BF16)
        zr.append(
            [put(zh_out.at[a, e], zh_in.at[a, 4 - e], at_zh(e)) for e in (1, 2, 3)]
        )
    for a in (0, 1):
        for copy in zr[a]:
            copy.wait_recv()
        total = piece[a, 0]
        for e in (1, 2, 3):
            total = total + zh_in[a, e].astype(F32)
        piece[a, 0] = total
        outs[a][...] = jnp.concatenate(
            [piece[a, 0, pl.ds(10 * j, 10), :] for j in range(6)], axis=1
        ).astype(BF16)
    for copy in started:
        copy.wait_send()


def on_device(tokens, weight_in, weight_out, mask_in, mask_out, grad_out):
    vmem = pl.BlockSpec(memory_space=pltpu.VMEM)
    smem = pl.BlockSpec(memory_space=pltpu.SMEM)
    hbm = pl.BlockSpec(memory_space=pl.ANY)
    shape = jax.ShapeDtypeStruct(tokens.shape, BF16)
    return pl.pallas_call(
        kernel,
        out_shape=(shape, shape),
        in_specs=[smem, smem, vmem, vmem, hbm, hbm],
        out_specs=(vmem, vmem),
        scratch_shapes=[
            pltpu.VMEM((768, 768), BF16),
            pltpu.VMEM((768, 768), BF16),
            pltpu.VMEM((2, 4, 2, 4, 64, 128), BF16),
            pltpu.VMEM((2, 64, 128), F32),
            pltpu.VMEM((1920, 128), F32),
            pltpu.VMEM((320, 768), BF16),
            pltpu.VMEM((2, PARTS, 4, ROWS, 128), F32),
            pltpu.VMEM((2, PARTS, 4, ROWS, 128), BF16),
            pltpu.VMEM((2, PARTS, 4, ROWS, 128), BF16),
            pltpu.VMEM((2, PARTS, 4, SHARE, 128), F32),
            pltpu.VMEM((2, PARTS, 4, SHARE, 128), BF16),
            pltpu.VMEM((2, PARTS, 4, SHARE, 128), BF16),
            pltpu.VMEM((PARTS, SHARE, 128), F32),
            pltpu.VMEM((2, PARTS, 4, 4, SHARE, 128), BF16),
            pltpu.VMEM((320, 768), F32),
            pltpu.VMEM((2, 4, 240, 128), F32),
            pltpu.VMEM((2, 4, 240, 128), F32),
            pltpu.VMEM((2, 4, 240, 128), BF16),
            pltpu.VMEM((2, 4, 240, 128), BF16),
            pltpu.VMEM((2, 4, 240, 128), F32),
            pltpu.VMEM((2, 4, 64, 128), F32),
            pltpu.VMEM((2, 4, 64, 128), BF16),
            pltpu.VMEM((2, 4, 64, 128), BF16),
            pltpu.SemaphoreType.DMA((2,)),
            pltpu.SemaphoreType.DMA((N_SEMS,)),
            pltpu.SemaphoreType.DMA((N_SEMS,)),
        ],
        compiler_params=pltpu.CompilerParams(
            collective_id=0, has_side_effects=True, vmem_limit_bytes=48 * 2**20
        ),
    )(mask_in, mask_out, tokens, grad_out, weight_in, weight_out)


def solution(mesh):
    placed = (
        P("col", "row"),
        P("row", "col"),
        P("col", "row"),
        P("row", "col"),
        P("col", "row"),
        P("col", "row"),
    )
    return jax.shard_map(
        on_device,
        mesh=mesh,
        in_specs=placed,
        out_specs=(P("col", "row"), P("col", "row")),
        check_vma=False,
    )
```

```python
import jax
import jax.numpy as jnp
from jax import lax
from jax.experimental import pallas as pl
from jax.experimental.pallas import tpu as pltpu
from jax.sharding import PartitionSpec as P

F32, BF16 = jnp.float32, jnp.bfloat16
MESH = pl.DeviceIdType.MESH
PLACES = (0, 1, 3, 2)
ORDER = (
    (1, 0, 0), (1, 1, 0), (0, 0, 1), (0, 0, 2), (0, 0, 3), (1, 0, 1), (0, 1, 1), (1, 0, 2),
    (0, 1, 2), (1, 0, 3), (0, 1, 3), (1, 1, 1), (2, 0, 0), (1, 1, 2), (1, 1, 3), (2, 1, 0),
    (2, 0, 1), (3, 0, 0), (2, 0, 2), (3, 1, 0), (2, 0, 3), (2, 1, 1), (3, 0, 1), (2, 1, 2),
    (4, 0, 0), (3, 0, 2), (2, 1, 3), (4, 1, 0), (3, 0, 3), (3, 1, 1), (4, 0, 1), (3, 1, 2),
    (5, 0, 0), (4, 0, 2), (3, 1, 3), (5, 1, 0), (6, 0, 0), (4, 0, 3), (4, 1, 1), (6, 1, 0),
    (5, 0, 1), (4, 1, 2), (5, 0, 2), (6, 0, 1), (4, 1, 3), (5, 0, 3), (6, 0, 2), (5, 1, 1),
    (6, 0, 3), (5, 1, 2), (6, 1, 1), (5, 1, 3), (6, 1, 2), (6, 1, 3), (7, 0, 0), (7, 1, 0),
)
N_SEMS = 34 + 8 * 21 + 20


def nn(a, b):
    return jnp.dot(a, b, preferred_element_type=F32)


def nt(a, b):
    return lax.dot_general(a, b, (((1,), (1,)), ((), ())), preferred_element_type=F32)


def lanes_to_rows(v):
    return jnp.concatenate(
        [v[:, 128 * j : 128 * (j + 1)] for j in range(v.shape[1] // 128)], axis=0
    )


def sigmoid_2u(v):
    u = 0.7978845608028654 * (v + 0.044715 * (v * v * v))
    return 1.0 / (1.0 + jnp.exp(jnp.minimum(-2.0 * u, 80.0)))


def kernel(
    mask_in_hbm, mask_out_hbm, tok_hbm, grad_hbm, w_in_hbm, w_out_hbm, out, gtok,
    mask_in, mask_out, tok, grad, w_in, w_out, gath, pack, unp, part_f, part_b, y_in,
    half_f, half_b, z_in, pre_s, hid, sib_out, sib_in, x_out, x_in, mine, piece, zh_out, zh_in,
    load_sem, send, recv,
):
    r, c = lax.axis_index("row"), lax.axis_index("col")
    zl, y = r // 4, r % 4
    zh, x, k = c // 8, (c // 2) % 4, c % 2

    def at_y(d):
        return {"row": zl * 4 + (y + d) % 4}

    def at_zl(d):
        return {"row": ((zl + d) % 4) * 4 + y}

    def at_x(d):
        return {"col": zh * 8 + ((x + d) % 4) * 2 + k}

    def at_zh(d):
        return {"col": ((zh + d) % 4) * 8 + x * 2 + k}

    sibling = {"col": zh * 8 + x * 2 + (1 - k)}

    barrier = pltpu.get_barrier_semaphore()
    peers = [at_zh(1), at_zh(3)]
    for d in (2, 1, 3):
        peers += [at_x(d), at_y(d), at_zl(d)]
    peers.append(sibling)
    for peer in peers:
        pl.semaphore_signal(barrier, inc=1, device_id=peer, device_id_type=MESH)

    loads = []
    for src, dst in (
        (tok_hbm, tok),
        (grad_hbm, grad),
        (mask_in_hbm, mask_in),
        (mask_out_hbm, mask_out),
        (w_in_hbm, w_in),
        (w_out_hbm, w_out),
    ):
        loads.append(pltpu.make_async_copy(src, dst, load_sem.at[len(loads)]))
        loads[-1].start()

    started = []

    def put(src, dst, peer):
        i = len(started)
        copy = pltpu.make_async_remote_copy(
            src_ref=src, dst_ref=dst, send_sem=send.at[i], recv_sem=recv.at[i],
            device_id=peer, device_id_type=MESH,
        )
        copy.start()
        started.append(copy)
        return copy

    def arrive(copies):
        for copy in copies:
            copy.wait_recv()

    for a, v in ((0, tok), (1, grad)):
        loads[a].wait()
        v = v[...].astype(F32)
        pack[a] = jnp.zeros((64, 128), F32)
        for j in range(6):
            pack[a, pl.ds(j, 10, stride=6), :] = v[:, 128 * j : 128 * (j + 1)]
        gath[a, 0, 0, 0] = pack[a].astype(BF16)
        for e in range(4):
            piece[a, e, pl.ds(56, 8), :] = jnp.zeros((8, 128), F32)
    pl.semaphore_wait(barrier, len(peers))

    near, far, xs, sibs = {}, {}, {}, {}

    def spread(a, lo, hi):
        src = gath.at[a, 0, 0, pl.ds(lo, hi - lo)]
        for d in (1, 3, 2):
            dst = gath.at[a, 4 - d, 0, pl.ds(lo, hi - lo)]
            xs.setdefault((a, 4 - d), []).append(put(src, dst, at_x(d)))

    for a in (0, 1):
        own = gath.at[a, 0, 0, 0]
        near[a] = [put(own, gath.at[a, 0, 0, 2], at_zh(1)), put(own, gath.at[a, 0, 0, 1], at_zh(3))]
    for a in (0, 1):
        spread(a, 0, 1)
    for load in loads[2:]:
        load.wait()
    for w, mask in ((w_in, mask_in), (w_out, mask_out)):
        for i in range(6):
            rows = slice(128 * i, 128 * (i + 1))
            for j in range(6):
                cols = slice(128 * j, 128 * (j + 1))
                keep = mask[i, j].astype(F32)
                w[rows, cols] = (w[rows, cols].astype(F32) * keep).astype(BF16)
    for a in (0, 1):
        arrive(near[a])
        top, low = pl.ds(0, 32), pl.ds(32, 32)
        far[a] = [
            put(gath.at[a, 0, 0, 1, top], gath.at[a, 0, 0, 3, top], at_zh(3)),
            put(gath.at[a, 0, 0, 2, low], gath.at[a, 0, 0, 3, low], at_zh(1)),
        ]
        spread(a, 1, 3)
    for a in (0, 1):
        arrive(far[a])
        sibs[a, 0] = put(gath.at[a, 0, 0], gath.at[a, 0, 1], sibling)
        spread(a, 3, 4)

    ys, zls, gz, gy, pairs, xr, zr = {}, {}, {}, {}, {}, {}, {}

    def to_sibling(a, d):
        arrive(xs[a, d])
        sibs[a, d] = put(gath.at[a, d, 0], gath.at[a, d, 1], sibling)

    def first_product(a, d):
        arrive([sibs[a, d]])
        for s in range(8):
            unp[a, pl.ds(60 * s, 60), :] = gath[a, d, s // 4, s % 4].astype(F32)[:60]
        left = jnp.concatenate(
            [unp[a, pl.ds(j, 80, stride=6), :].astype(BF16) for j in range(6)], axis=1
        )
        value = nn(left, w_in[...]) if a == 0 else nt(left, w_out[...])
        rows = jnp.concatenate([lanes_to_rows(value), jnp.zeros((32, 128), F32)], axis=0)
        for g in range(4):
            part = rows[128 * g : 128 * (g + 1)]
            part_f[a, d, g] = part
            part_b[a, d, g] = part.astype(BF16)
        ys[a, d] = [
            put(part_b.at[a, d, (y + e) % 4], y_in.at[a, d, 4 - e], at_y(e)) for e in (1, 3, 2)
        ]

    def sum_over_y(a, d):
        arrive(ys[a, d])
        total = part_f[a, d, y]
        for e in (1, 2, 3):
            total = total + y_in[a, d, e].astype(F32)
        for q in range(4):
            rows = total[32 * q : 32 * (q + 1)]
            half_f[a, d, q] = rows
            half_b[a, d, q] = rows.astype(BF16)
        zls[a, d] = [
            put(half_b.at[a, d, (zl + e) % 4], z_in.at[a, d, 4 - e], at_zl(e)) for e in (2, 1, 3)
        ]

    def activate(a, d):
        arrive(zls[a, d])
        total = half_f[a, d, zl]
        for e in (1, 2, 3):
            total = total + z_in[a, d, e].astype(F32)
        if a == 0:
            pre_s[d] = total
            value = total * sigmoid_2u(total)
        else:
            v = pre_s[d]
            s = sigmoid_2u(v)
            slope = 1.5957691216057308 * (1.0 + 0.134145 * (v * v))
            value = (s + v * (s * (1.0 - s)) * slope) * total
        hid[a, d, y, zl] = value.astype(BF16)
        slot = hid.at[a, d, y, zl]
        gz[a, d] = [put(slot, slot, at_zl(e)) for e in (1, 2, 3)]
        gy[a, d] = [put(slot, slot, at_y(e)) for e in (1, 3, 2)]

    def pass_on(a, d):
        for e in (1, 2, 3):
            arrive([gz[a, d][e - 1]])
            slot = hid.at[a, d, y, (zl + 4 - e) % 4]
            gy[a, d] += [put(slot, slot, at_y(f)) for f in (1, 3, 2)]

    def second_product(a, d):
        arrive(gy[a, d])
        rows = hid[a, d].reshape(512, 128)
        left = jnp.concatenate([rows[80 * j : 80 * (j + 1)] for j in range(6)], axis=1)
        value = nn(left, w_out[...]) if a == 0 else nt(left, w_in[...])
        mine[a, d] = lanes_to_rows(value[:40])
        sib_out[a, d] = lanes_to_rows(value[40:])
        pairs[a, d] = put(sib_out.at[a, d], sib_in.at[a, d], sibling)

    def sum_over_cores(a, d):
        arrive([pairs[a, d]])
        total = mine[a, d] + sib_in[a, d]
        if d:
            x_out[a, d] = total.astype(BF16)
            xr[a, d] = put(x_out.at[a, d], x_in.at[a, 4 - d], at_x(d))
        else:
            mine[a, 0] = total

    def sum_over_x(a, _):
        arrive([xr[a, d] for d in (1, 2, 3)])
        total = mine[a, 0]
        for d in (1, 2, 3):
            total = total + x_in[a, d].astype(F32)
        mine[a, 0] = total
        zr[a] = []
        for p in (3, 1, 2, 0):
            e = PLACES[p]
            for j in range(6):
                piece[a, p, pl.ds(10 * j, 10), :] = mine[a, 0, pl.ds(40 * j + 10 * p, 10), :]
            if e:
                zh_out[a, p] = piece[a, p].astype(BF16)
                zr[a].append(put(zh_out.at[a, p], zh_in.at[a, 4 - e], at_zh(e)))

    stages = (
        to_sibling, first_product, sum_over_y, activate, pass_on, second_product,
        sum_over_cores, sum_over_x,
    )
    for stage, a, d in ORDER:
        stages[stage](a, d)
    for a, ref in ((0, out), (1, gtok)):
        arrive(zr[a])
        total = piece[a, 0]
        for e in (1, 2, 3):
            total = total + zh_in[a, e].astype(F32)
        piece[a, 0] = total
        ref[...] = jnp.concatenate(
            [piece[a, 0, pl.ds(10 * j, 10), :] for j in range(6)], axis=1
        ).astype(BF16)
    for copy in started:
        copy.wait_send()


def on_device(tokens, weight_in, weight_out, mask_in, mask_out, grad_out):
    vmem = pl.BlockSpec(memory_space=pltpu.VMEM)
    hbm = pl.BlockSpec(memory_space=pltpu.HBM)
    shape = jax.ShapeDtypeStruct(tokens.shape, BF16)
    return pl.pallas_call(
        kernel,
        out_shape=(shape, shape),
        in_specs=[hbm] * 6,
        out_specs=(vmem, vmem),
        scratch_shapes=[
            pltpu.SMEM(mask_in.shape, jnp.int32),
            pltpu.SMEM(mask_out.shape, jnp.int32),
            pltpu.VMEM(tokens.shape, BF16),
            pltpu.VMEM(tokens.shape, BF16),
            pltpu.VMEM((768, 768), BF16),
            pltpu.VMEM((768, 768), BF16),
            pltpu.VMEM((2, 4, 2, 4, 64, 128), BF16),
            pltpu.VMEM((2, 64, 128), F32),
            pltpu.VMEM((2, 480, 128), F32),
            pltpu.VMEM((2, 4, 4, 128, 128), F32),
            pltpu.VMEM((2, 4, 4, 128, 128), BF16),
            pltpu.VMEM((2, 4, 4, 128, 128), BF16),
            pltpu.VMEM((2, 4, 4, 32, 128), F32),
            pltpu.VMEM((2, 4, 4, 32, 128), BF16),
            pltpu.VMEM((2, 4, 4, 32, 128), BF16),
            pltpu.VMEM((4, 32, 128), F32),
            pltpu.VMEM((2, 4, 4, 4, 32, 128), BF16),
            pltpu.VMEM((2, 4, 240, 128), F32),
            pltpu.VMEM((2, 4, 240, 128), F32),
            pltpu.VMEM((2, 4, 240, 128), BF16),
            pltpu.VMEM((2, 4, 240, 128), BF16),
            pltpu.VMEM((2, 4, 240, 128), F32),
            pltpu.VMEM((2, 4, 64, 128), F32),
            pltpu.VMEM((2, 4, 64, 128), BF16),
            pltpu.VMEM((2, 4, 64, 128), BF16),
            pltpu.SemaphoreType.DMA((6,)),
            pltpu.SemaphoreType.DMA((N_SEMS,)),
            pltpu.SemaphoreType.DMA((N_SEMS,)),
        ],
        compiler_params=pltpu.CompilerParams(
            collective_id=0, has_side_effects=True, vmem_limit_bytes=60 * 2**20
        ),
    )(mask_in, mask_out, tokens, grad_out, weight_in, weight_out)


def solution(mesh):
    placed = (
        P("col", "row"),
        P("row", "col"),
        P("col", "row"),
        P("row", "col"),
        P("col", "row"),
        P("col", "row"),
    )
    return jax.shard_map(
        on_device,
        mesh=mesh,
        in_specs=placed,
        out_specs=(P("col", "row"), P("col", "row")),
        check_vma=False,
    )
```

```python
import jax
import jax.numpy as jnp
from jax import lax
from jax.experimental import pallas as pl
from jax.experimental.pallas import tpu as pltpu
from jax.sharding import PartitionSpec as P

F32, BF16 = jnp.float32, jnp.bfloat16
MESH = pl.DeviceIdType.MESH
PLACES = (0, 1, 3, 2)
ORDER = (
    (2, 0, 0), (2, 1, 0), (3, 0, 0), (3, 1, 0), (0, 0, 0), (0, 1, 0), (4, 0, 0), (2, 0, 1),
    (2, 0, 2), (3, 0, 1), (4, 1, 0), (2, 1, 1), (1, 0, 3), (3, 0, 2), (2, 1, 2), (1, 1, 3),
    (3, 1, 1), (3, 1, 2), (5, 0, 0), (2, 0, 3), (5, 1, 0), (4, 0, 1), (2, 1, 3), (3, 0, 3),
    (4, 0, 2), (3, 1, 3), (6, 0, 0), (4, 1, 1), (6, 1, 0), (4, 1, 2), (5, 0, 1), (5, 0, 2),
    (4, 0, 3), (5, 1, 1), (4, 1, 3), (5, 1, 2), (7, 0, 0), (6, 0, 1), (7, 1, 0), (6, 0, 2),
    (8, 0, 0), (5, 0, 3), (8, 1, 0), (6, 1, 1), (5, 1, 3), (6, 1, 2), (7, 0, 1), (9, 0, 0),
    (7, 0, 2), (6, 0, 3), (8, 0, 1), (9, 1, 0), (7, 1, 1), (8, 0, 2), (6, 1, 3), (7, 1, 2),
    (8, 1, 1), (8, 1, 2), (9, 0, 1), (7, 0, 3), (9, 0, 2), (7, 1, 3), (8, 0, 3), (9, 1, 1),
    (8, 1, 3), (9, 1, 2), (9, 0, 3), (9, 1, 3),
)
N_SEMS = 40 + 8 * 21 + 38


def nn(a, b):
    return jnp.dot(a, b, preferred_element_type=F32)


def nt(a, b):
    return lax.dot_general(a, b, (((1,), (1,)), ((), ())), preferred_element_type=F32)


def lanes_to_rows(v):
    return jnp.concatenate(
        [v[:, 128 * j : 128 * (j + 1)] for j in range(v.shape[1] // 128)], axis=0
    )


def sigmoid_2u(v):
    u = 0.7978845608028654 * (v + 0.044715 * (v * v * v))
    return 1.0 / (1.0 + jnp.exp(jnp.minimum(-2.0 * u, 80.0)))


def kernel(
    mask_in_hbm, mask_out_hbm, tok_hbm, grad_hbm, w_in_hbm, w_out_hbm, out, gtok,
    mask_in, mask_out, tok, grad, w_in, w_out, gath, pack, unp, part_f, part_b, y_in,
    half_f, half_b, z_in, pre_s, hid, sib_out, sib_in, x_out, x_in, mine, piece, zh_out, zh_in,
    load_sem, send, recv,
):
    r, c = lax.axis_index("row"), lax.axis_index("col")
    zl, y = r // 4, r % 4
    zh, x, k = c // 8, (c // 2) % 4, c % 2

    def at_y(d):
        return {"row": zl * 4 + (y + d) % 4}

    def at_zl(d):
        return {"row": ((zl + d) % 4) * 4 + y}

    def at_x(d):
        return {"col": zh * 8 + ((x + d) % 4) * 2 + k}

    def at_zh(d):
        return {"col": ((zh + d) % 4) * 8 + x * 2 + k}

    sibling = {"col": zh * 8 + x * 2 + (1 - k)}

    barrier = pltpu.get_barrier_semaphore()
    peers = [at_zh(1), at_zh(3)]
    for d in (2, 1, 3):
        peers += [at_x(d), at_y(d), at_zl(d)]
    peers.append(sibling)
    for peer in peers:
        pl.semaphore_signal(barrier, inc=1, device_id=peer, device_id_type=MESH)

    loads = []
    for src, dst in (
        (tok_hbm, tok),
        (grad_hbm, grad),
        (mask_in_hbm, mask_in),
        (mask_out_hbm, mask_out),
        (w_in_hbm, w_in),
        (w_out_hbm, w_out),
    ):
        loads.append(pltpu.make_async_copy(src, dst, load_sem.at[len(loads)]))
        loads[-1].start()

    started = []

    def put(src, dst, peer):
        i = len(started)
        copy = pltpu.make_async_remote_copy(
            src_ref=src, dst_ref=dst, send_sem=send.at[i], recv_sem=recv.at[i],
            device_id=peer, device_id_type=MESH,
        )
        copy.start()
        started.append(copy)
        return copy

    def arrive(copies):
        for copy in copies:
            copy.wait_recv()

    for a, v in ((0, tok), (1, grad)):
        loads[a].wait()
        v = v[...].astype(F32)
        pack[a] = jnp.zeros((64, 128), F32)
        for j in range(6):
            pack[a, pl.ds(j, 10, stride=6), :] = v[:, 128 * j : 128 * (j + 1)]
        gath[a, 0, 0, 0] = pack[a].astype(BF16)
        for p in range(4):
            for e in range(4):
                piece[a, p, e, pl.ds(56, 8), :] = jnp.zeros((8, 128), F32)
    pl.semaphore_wait(barrier, len(peers))

    near, far, xs, sibs = {}, {}, {}, {}
    ys, zls, gz, gy, pairs, xr, zr = {}, {}, {}, {}, {}, {}, {0: [], 1: []}

    def spread(a, p):
        xs[a, p] = [put(gath.at[a, p, 0, 0], gath.at[a, p, 0, 4 - e], at_x(e)) for e in (2, 1, 3)]

    def from_near(a, _):
        top, low = pl.ds(0, 32), pl.ds(32, 32)
        arrive(near[a][1:])
        far[a] = [put(gath.at[a, 1, 0, 0, top], gath.at[a, 3, 0, 0, top], at_zh(3))]
        arrive(near[a][:1])
        far[a].append(put(gath.at[a, 2, 0, 0, low], gath.at[a, 3, 0, 0, low], at_zh(1)))
        spread(a, 1)
        spread(a, 2)

    def from_far(a, p):
        arrive(far[a])
        spread(a, p)

    def to_sibling(a, p):
        arrive(xs[a, p])
        sibs[a, p] = put(gath.at[a, p, 0], gath.at[a, p, 1], sibling)

    for a in (0, 1):
        own = gath.at[a, 0, 0, 0]
        near[a] = [put(own, gath.at[a, 2, 0, 0], at_zh(1)), put(own, gath.at[a, 1, 0, 0], at_zh(3))]
    for a in (0, 1):
        spread(a, 0)
    for load in loads[2:]:
        load.wait()
    for w, mask in ((w_in, mask_in), (w_out, mask_out)):
        for i in range(6):
            rows = slice(128 * i, 128 * (i + 1))
            for j in range(6):
                cols = slice(128 * j, 128 * (j + 1))
                keep = mask[i, j].astype(F32)
                w[rows, cols] = (w[rows, cols].astype(F32) * keep).astype(BF16)

    def first_product(a, d):
        arrive([sibs[a, d]])
        for s in range(8):
            unp[a, pl.ds(60 * s, 60), :] = gath[a, d, s // 4, s % 4].astype(F32)[:60]
        left = jnp.concatenate(
            [unp[a, pl.ds(j, 80, stride=6), :].astype(BF16) for j in range(6)], axis=1
        )
        value = nn(left, w_in[...]) if a == 0 else nt(left, w_out[...])
        rows = jnp.concatenate([lanes_to_rows(value), jnp.zeros((32, 128), F32)], axis=0)
        for g in range(4):
            part = rows[128 * g : 128 * (g + 1)]
            part_f[a, d, g] = part
            part_b[a, d, g] = part.astype(BF16)
        ys[a, d] = [
            put(part_b.at[a, d, (y + e) % 4], y_in.at[a, d, 4 - e], at_y(e)) for e in (2, 1, 3)
        ]

    def sum_over_y(a, d):
        arrive(ys[a, d])
        total = part_f[a, d, y]
        for e in (1, 2, 3):
            total = total + y_in[a, d, e].astype(F32)
        for q in range(4):
            rows = total[32 * q : 32 * (q + 1)]
            half_f[a, d, q] = rows
            half_b[a, d, q] = rows.astype(BF16)
        zls[a, d] = [
            put(half_b.at[a, d, (zl + e) % 4], z_in.at[a, d, 4 - e], at_zl(e)) for e in (2, 1, 3)
        ]

    def activate(a, d):
        arrive(zls[a, d])
        total = half_f[a, d, zl]
        for e in (1, 2, 3):
            total = total + z_in[a, d, e].astype(F32)
        if a == 0:
            pre_s[d] = total
            value = total * sigmoid_2u(total)
        else:
            v = pre_s[d]
            s = sigmoid_2u(v)
            slope = 1.5957691216057308 * (1.0 + 0.134145 * (v * v))
            value = (s + v * (s * (1.0 - s)) * slope) * total
        hid[a, d, y, zl] = value.astype(BF16)
        slot = hid.at[a, d, y, zl]
        gz[a, d] = [put(slot, slot, at_zl(e)) for e in (1, 2, 3)]
        gy[a, d] = [put(slot, slot, at_y(e)) for e in (1, 3, 2)]

    def pass_on(a, d):
        for e in (1, 2, 3):
            arrive([gz[a, d][e - 1]])
            slot = hid.at[a, d, y, (zl + 4 - e) % 4]
            gy[a, d] += [put(slot, slot, at_y(f)) for f in (1, 3, 2)]

    def second_product(a, d):
        arrive(gy[a, d])
        rows = hid[a, d].reshape(512, 128)
        left = jnp.concatenate([rows[80 * j : 80 * (j + 1)] for j in range(6)], axis=1)
        value = nn(left, w_out[...]) if a == 0 else nt(left, w_in[...])
        mine[a, d] = lanes_to_rows(value[:40])
        sib_out[a, d] = lanes_to_rows(value[40:])
        pairs[a, d] = put(sib_out.at[a, d], sib_in.at[a, d], sibling)

    def sum_over_cores(a, d):
        arrive([pairs[a, d]])
        mine[a, d] = mine[a, d] + sib_in[a, d]
        xr[a, d] = []
        for e in (2, 1, 3, 0):
            for j in range(6):
                piece[a, d, e, pl.ds(10 * j, 10), :] = mine[a, d, pl.ds(40 * j + 10 * e, 10), :]
            if e:
                x_out[a, d, e] = piece[a, d, e].astype(BF16)
                xr[a, d].append(put(x_out.at[a, d, e], x_in.at[a, d, 4 - e], at_x(e)))

    def sum_over_x(a, p):
        arrive(xr[a, p])
        total = piece[a, p, 0]
        for e in (1, 2, 3):
            total = total + x_in[a, p, e].astype(F32)
        e = PLACES[p]
        if e:
            zh_out[a, e] = total.astype(BF16)
            zr[a].append(put(zh_out.at[a, e], zh_in.at[a, 4 - e], at_zh(e)))
        else:
            piece[a, 0, 0] = total

    stages = (
        from_near, from_far, to_sibling, first_product, sum_over_y, activate, pass_on,
        second_product, sum_over_cores, sum_over_x,
    )
    for stage, a, p in ORDER:
        stages[stage](a, p)
    for a, ref in ((0, out), (1, gtok)):
        arrive(zr[a])
        total = piece[a, 0, 0]
        for e in (1, 2, 3):
            total = total + zh_in[a, e].astype(F32)
        piece[a, 0, 0] = total
        ref[...] = jnp.concatenate(
            [piece[a, 0, 0, pl.ds(10 * j, 10), :] for j in range(6)], axis=1
        ).astype(BF16)
    for copy in started:
        copy.wait_send()


def on_device(tokens, weight_in, weight_out, mask_in, mask_out, grad_out):
    vmem = pl.BlockSpec(memory_space=pltpu.VMEM)
    hbm = pl.BlockSpec(memory_space=pltpu.HBM)
    shape = jax.ShapeDtypeStruct(tokens.shape, BF16)
    return pl.pallas_call(
        kernel,
        out_shape=(shape, shape),
        in_specs=[hbm] * 6,
        out_specs=(vmem, vmem),
        scratch_shapes=[
            pltpu.SMEM(mask_in.shape, jnp.int32),
            pltpu.SMEM(mask_out.shape, jnp.int32),
            pltpu.VMEM(tokens.shape, BF16),
            pltpu.VMEM(tokens.shape, BF16),
            pltpu.VMEM((768, 768), BF16),
            pltpu.VMEM((768, 768), BF16),
            pltpu.VMEM((2, 4, 2, 4, 64, 128), BF16),
            pltpu.VMEM((2, 64, 128), F32),
            pltpu.VMEM((2, 480, 128), F32),
            pltpu.VMEM((2, 4, 4, 128, 128), F32),
            pltpu.VMEM((2, 4, 4, 128, 128), BF16),
            pltpu.VMEM((2, 4, 4, 128, 128), BF16),
            pltpu.VMEM((2, 4, 4, 32, 128), F32),
            pltpu.VMEM((2, 4, 4, 32, 128), BF16),
            pltpu.VMEM((2, 4, 4, 32, 128), BF16),
            pltpu.VMEM((4, 32, 128), F32),
            pltpu.VMEM((2, 4, 4, 4, 32, 128), BF16),
            pltpu.VMEM((2, 4, 240, 128), F32),
            pltpu.VMEM((2, 4, 240, 128), F32),
            pltpu.VMEM((2, 4, 4, 64, 128), BF16),
            pltpu.VMEM((2, 4, 4, 64, 128), BF16),
            pltpu.VMEM((2, 4, 240, 128), F32),
            pltpu.VMEM((2, 4, 4, 64, 128), F32),
            pltpu.VMEM((2, 4, 64, 128), BF16),
            pltpu.VMEM((2, 4, 64, 128), BF16),
            pltpu.SemaphoreType.DMA((6,)),
            pltpu.SemaphoreType.DMA((N_SEMS,)),
            pltpu.SemaphoreType.DMA((N_SEMS,)),
        ],
        compiler_params=pltpu.CompilerParams(
            collective_id=0, has_side_effects=True, vmem_limit_bytes=60 * 2**20
        ),
    )(mask_in, mask_out, tokens, grad_out, weight_in, weight_out)


def solution(mesh):
    placed = (
        P("col", "row"),
        P("row", "col"),
        P("col", "row"),
        P("row", "col"),
        P("col", "row"),
        P("col", "row"),
    )
    return jax.shard_map(
        on_device,
        mesh=mesh,
        in_specs=placed,
        out_specs=(P("col", "row"), P("col", "row")),
        check_vma=False,
    )
```

```python
import jax
import jax.numpy as jnp
from jax import lax
from jax.experimental import pallas as pl
from jax.experimental.pallas import tpu as pltpu
from jax.sharding import PartitionSpec as P

F32, BF16 = jnp.float32, jnp.bfloat16
MESH = pl.DeviceIdType.MESH
PLACES = (0, 1, 3, 2)
ORDER = (
    (2, 0, 0), (2, 1, 0), (3, 0, 0), (3, 1, 0), (0, 0, 0), (0, 1, 0), (4, 0, 0), (2, 0, 1),
    (2, 0, 2), (3, 0, 1), (4, 1, 0), (2, 1, 1), (1, 0, 3), (3, 0, 2), (2, 1, 2), (1, 1, 3),
    (3, 1, 1), (3, 1, 2), (5, 0, 0), (2, 0, 3), (5, 1, 0), (4, 0, 1), (2, 1, 3), (3, 0, 3),
    (4, 0, 2), (3, 1, 3), (6, 0, 0), (4, 1, 1), (6, 1, 0), (4, 1, 2), (5, 0, 1), (5, 0, 2),
    (4, 0, 3), (5, 1, 1), (4, 1, 3), (5, 1, 2), (7, 0, 0), (6, 0, 1), (7, 1, 0), (6, 0, 2),
    (8, 0, 0), (5, 0, 3), (8, 1, 0), (6, 1, 1), (5, 1, 3), (6, 1, 2), (7, 0, 1), (9, 0, 0),
    (7, 0, 2), (6, 0, 3), (8, 0, 1), (9, 1, 0), (7, 1, 1), (8, 0, 2), (6, 1, 3), (7, 1, 2),
    (8, 1, 1), (8, 1, 2), (9, 0, 1), (7, 0, 3), (9, 0, 2), (7, 1, 3), (8, 0, 3), (9, 1, 1),
    (8, 1, 3), (9, 1, 2), (9, 0, 3), (9, 1, 3),
)
NEAR, FAR, XS, SIB, YS, ZS, GZ, GY, PAIR, XR, ZR = range(11)


def nn(a, b):
    return jnp.dot(a, b, preferred_element_type=F32)


def nt(a, b):
    return lax.dot_general(a, b, (((1,), (1,)), ((), ())), preferred_element_type=F32)


def lanes_to_rows(v):
    return jnp.concatenate(
        [v[:, 128 * j : 128 * (j + 1)] for j in range(v.shape[1] // 128)], axis=0
    )


def sigmoid_2u(v):
    u = 0.7978845608028654 * (v + 0.044715 * (v * v * v))
    return 1.0 / (1.0 + jnp.exp(jnp.minimum(-2.0 * u, 80.0)))


def kernel(
    mask_in_hbm, mask_out_hbm, tok_hbm, grad_hbm, w_in_hbm, w_out_hbm, out,
    mask_in, mask_out, tok, grad, w_in, w_out, gath, pack, unp, part_f, part_b, y_in,
    half_f, half_b, z_in, pre_s, hid, sib_out, sib_in, x_out, x_in, mine, piece, zh_out, zh_in,
    load_sem, send, got_near, got_far, got_x, got_sib, got_y, got_z, got_gz, got_gy, got_pair, got_xr,
    got_zr,
):
    r, c = lax.axis_index("row"), lax.axis_index("col")
    zl, y = r // 4, r % 4
    zh, x, k = c // 8, (c // 2) % 4, c % 2

    def at_y(d):
        return {"row": zl * 4 + (y + d) % 4}

    def at_zl(d):
        return {"row": ((zl + d) % 4) * 4 + y}

    def at_x(d):
        return {"col": zh * 8 + ((x + d) % 4) * 2 + k}

    def at_zh(d):
        return {"col": ((zh + d) % 4) * 8 + x * 2 + k}

    sibling = {"col": zh * 8 + x * 2 + (1 - k)}

    barrier = pltpu.get_barrier_semaphore()
    peers = [at_zh(1), at_zh(3)]
    for d in (2, 1, 3):
        peers += [at_x(d), at_y(d), at_zl(d)]
    peers.append(sibling)
    for peer in peers:
        pl.semaphore_signal(barrier, inc=1, device_id=peer, device_id_type=MESH)

    loads = []
    for src, dst in (
        (tok_hbm, tok),
        (grad_hbm, grad),
        (mask_in_hbm, mask_in),
        (mask_out_hbm, mask_out),
        (w_in_hbm, w_in),
        (w_out_hbm, w_out),
    ):
        loads.append(pltpu.make_async_copy(src, dst, load_sem.at[len(loads)]))
        loads[-1].start()

    def put(src, dst, peer, kind, sem):
        pltpu.make_async_remote_copy(
            src_ref=src, dst_ref=dst, send_sem=send.at[kind], recv_sem=sem,
            device_id=peer, device_id_type=MESH,
        ).start()

    def arrive(ref, sem):
        pltpu.make_async_copy(ref, ref, sem).wait()

    for a, v in ((0, tok), (1, grad)):
        loads[a].wait()
        v = v[...].astype(F32)
        pack[a] = jnp.zeros((64, 128), F32)
        for j in range(6):
            pack[a, pl.ds(j, 10, stride=6), :] = v[:, 128 * j : 128 * (j + 1)]
        gath[a, 0, 0, 0] = pack[a].astype(BF16)
        for p in range(4):
            for e in range(4):
                piece[a, p, e, pl.ds(56, 8), :] = jnp.zeros((8, 128), F32)
    pl.semaphore_wait(barrier, len(peers))

    def spread(a, p):
        for e in (2, 1, 3):
            put(gath.at[a, p, 0, 0], gath.at[a, p, 0, 4 - e], at_x(e), XS, got_x.at[a, p])

    def from_near(a, _):
        top, low = pl.ds(0, 32), pl.ds(32, 32)
        far = gath.at[a, 3, 0, 0]
        arrive(gath.at[a, 1, 0, 0], got_near.at[a, 1])
        put(gath.at[a, 1, 0, 0, top], far.at[top], at_zh(3), FAR, got_far.at[a])
        arrive(gath.at[a, 2, 0, 0], got_near.at[a, 0])
        put(gath.at[a, 2, 0, 0, low], far.at[low], at_zh(1), FAR, got_far.at[a])
        spread(a, 1)
        spread(a, 2)

    def from_far(a, p):
        arrive(gath.at[a, 3, 0, 0], got_far.at[a])
        spread(a, p)

    def to_sibling(a, p):
        arrive(gath.at[a, p, 0, pl.ds(1, 3)], got_x.at[a, p])
        put(gath.at[a, p, 0], gath.at[a, p, 1], sibling, SIB, got_sib.at[a, p])

    for a in (0, 1):
        own = gath.at[a, 0, 0, 0]
        put(own, gath.at[a, 2, 0, 0], at_zh(1), NEAR, got_near.at[a, 0])
        put(own, gath.at[a, 1, 0, 0], at_zh(3), NEAR, got_near.at[a, 1])
    for a in (0, 1):
        spread(a, 0)
    for load in loads[2:]:
        load.wait()
    for w, mask in ((w_in, mask_in), (w_out, mask_out)):
        for i in range(6):
            rows = slice(128 * i, 128 * (i + 1))
            for j in range(6):
                cols = slice(128 * j, 128 * (j + 1))
                keep = mask[i, j].astype(F32)
                w[rows, cols] = (w[rows, cols].astype(F32) * keep).astype(BF16)

    def first_product(a, d):
        arrive(gath.at[a, d, 1], got_sib.at[a, d])
        for s in range(8):
            unp[a, pl.ds(60 * s, 60), :] = gath[a, d, s // 4, s % 4].astype(F32)[:60]
        left = jnp.concatenate(
            [unp[a, pl.ds(j, 80, stride=6), :].astype(BF16) for j in range(6)], axis=1
        ).astype(BF16)
        value = nn(left, w_in[...]) if a == 0 else nt(left, w_out[...])
        rows = jnp.concatenate([lanes_to_rows(value), jnp.zeros((32, 128), F32)], axis=0)
        for g in range(4):
            part = rows[128 * g : 128 * (g + 1)]
            part_f[a, d, g] = part
            part_b[a, d, g] = part.astype(BF16)
        for e in (2, 1, 3):
            put(part_b.at[a, d, (y + e) % 4], y_in.at[a, d, 4 - e], at_y(e), YS, got_y.at[a, d])

    def sum_over_y(a, d):
        arrive(y_in.at[a, d, pl.ds(1, 3)], got_y.at[a, d])
        total = part_f[a, d, y]
        for e in (1, 2, 3):
            total = total + y_in[a, d, e].astype(F32)
        for q in range(4):
            rows = total[32 * q : 32 * (q + 1)]
            half_f[a, d, q] = rows
            half_b[a, d, q] = rows.astype(BF16)
        for e in (2, 1, 3):
            put(half_b.at[a, d, (zl + e) % 4], z_in.at[a, d, 4 - e], at_zl(e), ZS, got_z.at[a, d])

    def activate(a, d):
        arrive(z_in.at[a, d, pl.ds(1, 3)], got_z.at[a, d])
        total = half_f[a, d, zl]
        for e in (1, 2, 3):
            total = total + z_in[a, d, e].astype(F32)
        if a == 0:
            pre_s[d] = total
            value = total * sigmoid_2u(total)
        else:
            v = pre_s[d]
            s = sigmoid_2u(v)
            slope = 1.5957691216057308 * (1.0 + 0.134145 * (v * v))
            value = (s + v * (s * (1.0 - s)) * slope) * total
        hid[a, d, y, zl] = value.astype(BF16)
        slot = hid.at[a, d, y, zl]
        for e in (1, 2, 3):
            put(slot, slot, at_zl(e), GZ, got_gz.at[a, d, e])
        for e in (1, 3, 2):
            put(slot, slot, at_y(e), GY, got_gy.at[a, d])

    def pass_on(a, d):
        for e in (1, 2, 3):
            slot = hid.at[a, d, y, (zl + 4 - e) % 4]
            arrive(slot, got_gz.at[a, d, e])
            for f in (1, 3, 2):
                put(slot, slot, at_y(f), GY, got_gy.at[a, d])

    def second_product(a, d):
        arrive(hid.at[a, d, pl.ds(0, 3)], got_gy.at[a, d])
        rows = hid[a, d].reshape(512, 128)
        left = jnp.concatenate([rows[80 * j : 80 * (j + 1)] for j in range(6)], axis=1)
        value = nn(left, w_out[...]) if a == 0 else nt(left, w_in[...])
        mine[a, d] = lanes_to_rows(value[:40])
        sib_out[a, d] = lanes_to_rows(value[40:])
        put(sib_out.at[a, d], sib_in.at[a, d], sibling, PAIR, got_pair.at[a, d])

    def sum_over_cores(a, d):
        arrive(sib_in.at[a, d], got_pair.at[a, d])
        mine[a, d] = mine[a, d] + sib_in[a, d]
        for e in (2, 1, 3, 0):
            for j in range(6):
                piece[a, d, e, pl.ds(10 * j, 10), :] = mine[a, d, pl.ds(40 * j + 10 * e, 10), :]
            if e:
                x_out[a, d, e] = piece[a, d, e].astype(BF16)
                put(x_out.at[a, d, e], x_in.at[a, d, 4 - e], at_x(e), XR, got_xr.at[a, d])

    def sum_over_x(a, p):
        arrive(x_in.at[a, p, pl.ds(1, 3)], got_xr.at[a, p])
        total = piece[a, p, 0]
        for e in (1, 2, 3):
            total = total + x_in[a, p, e].astype(F32)
        e = PLACES[p]
        if e:
            zh_out[a, e] = total.astype(BF16)
            put(zh_out.at[a, e], zh_in.at[a, 4 - e], at_zh(e), ZR, got_zr.at[a])
        else:
            piece[a, 0, 0] = total

    stages = (
        from_near, from_far, to_sibling, first_product, sum_over_y, activate, pass_on,
        second_product, sum_over_cores, sum_over_x,
    )
    for stage, a, p in ORDER:
        stages[stage](a, p)
    for a in (0, 1):
        arrive(zh_in.at[a, pl.ds(1, 3)], got_zr.at[a])
        total = piece[a, 0, 0]
        for e in (1, 2, 3):
            total = total + zh_in[a, e].astype(F32)
        piece[a, 0, 0] = total
        out[a] = jnp.concatenate(
            [piece[a, 0, 0, pl.ds(10 * j, 10), :] for j in range(6)], axis=1
        ).astype(BF16)
    every = slice(None)
    for kind, ref in (
        (NEAR, gath.at[0, 0, 0]),
        (FAR, gath.at[0, 0, 0, pl.ds(0, 2)]),
        (XS, gath.at[every, every, 0, pl.ds(1, 3)]),
        (SIB, gath.at[every, every, 0]),
        (YS, y_in.at[every, every, pl.ds(1, 3)]),
        (ZS, z_in.at[every, every, pl.ds(1, 3)]),
        (GZ, z_in.at[every, every, pl.ds(1, 3)]),
        (GY, hid.at[every, every, pl.ds(0, 3)]),
        (PAIR, sib_in),
        (XR, x_in.at[every, every, pl.ds(1, 3)]),
        (ZR, zh_in.at[every, pl.ds(1, 3)]),
    ):
        arrive(ref, send.at[kind])


def on_device(tokens, weight_in, weight_out, mask_in, mask_out, grad_out):
    vmem = pl.BlockSpec(memory_space=pltpu.VMEM)
    hbm = pl.BlockSpec(memory_space=pltpu.HBM)
    shape = jax.ShapeDtypeStruct((2,) + tokens.shape, BF16)
    o = pl.pallas_call(
        kernel,
        out_shape=shape,
        in_specs=[hbm] * 6,
        out_specs=vmem,
        scratch_shapes=[
            pltpu.SMEM(mask_in.shape, jnp.int32),
            pltpu.SMEM(mask_out.shape, jnp.int32),
            pltpu.VMEM(tokens.shape, BF16),
            pltpu.VMEM(tokens.shape, BF16),
            pltpu.VMEM((768, 768), BF16),
            pltpu.VMEM((768, 768), BF16),
            pltpu.VMEM((2, 4, 2, 4, 64, 128), BF16),
            pltpu.VMEM((2, 64, 128), F32),
            pltpu.VMEM((2, 480, 128), F32),
            pltpu.VMEM((2, 4, 4, 128, 128), F32),
            pltpu.VMEM((2, 4, 4, 128, 128), BF16),
            pltpu.VMEM((2, 4, 4, 128, 128), BF16),
            pltpu.VMEM((2, 4, 4, 32, 128), F32),
            pltpu.VMEM((2, 4, 4, 32, 128), BF16),
            pltpu.VMEM((2, 4, 4, 32, 128), BF16),
            pltpu.VMEM((4, 32, 128), F32),
            pltpu.VMEM((2, 4, 4, 4, 32, 128), BF16),
            pltpu.VMEM((2, 4, 240, 128), F32),
            pltpu.VMEM((2, 4, 240, 128), F32),
            pltpu.VMEM((2, 4, 4, 64, 128), BF16),
            pltpu.VMEM((2, 4, 4, 64, 128), BF16),
            pltpu.VMEM((2, 4, 240, 128), F32),
            pltpu.VMEM((2, 4, 4, 64, 128), F32),
            pltpu.VMEM((2, 4, 64, 128), BF16),
            pltpu.VMEM((2, 4, 64, 128), BF16),
            pltpu.SemaphoreType.DMA((6,)),
            pltpu.SemaphoreType.DMA((11,)),
            pltpu.SemaphoreType.DMA((2, 2)),
            pltpu.SemaphoreType.DMA((2,)),
            pltpu.SemaphoreType.DMA((2, 4)),
            pltpu.SemaphoreType.DMA((2, 4)),
            pltpu.SemaphoreType.DMA((2, 4)),
            pltpu.SemaphoreType.DMA((2, 4)),
            pltpu.SemaphoreType.DMA((2, 4, 4)),
            pltpu.SemaphoreType.DMA((2, 4)),
            pltpu.SemaphoreType.DMA((2, 4)),
            pltpu.SemaphoreType.DMA((2, 4)),
            pltpu.SemaphoreType.DMA((2,)),
        ],
        compiler_params=pltpu.CompilerParams(
            collective_id=0, has_side_effects=True, vmem_limit_bytes=60 * 2**20
        ),
    )(mask_in, mask_out, tokens, grad_out, weight_in, weight_out)
    return o[0], o[1]


def solution(mesh):
    placed = (
        P("col", "row"),
        P("row", "col"),
        P("col", "row"),
        P("row", "col"),
        P("col", "row"),
        P("col", "row"),
    )
    return jax.shard_map(
        on_device,
        mesh=mesh,
        in_specs=placed,
        out_specs=(P("col", "row"), P("col", "row")),
        check_vma=False,
    )
```

```python
import jax
import jax.numpy as jnp
from jax import lax
from jax.experimental import pallas as pl
from jax.experimental.pallas import tpu as pltpu
from jax.sharding import PartitionSpec as P

F32, BF16 = jnp.float32, jnp.bfloat16
MESH = pl.DeviceIdType.MESH
PLACES = (0, 1, 3, 2)
ORDER = (
    (3, 0, 0), (0, 0, 0), (4, 0, 0), (0, 1, 0), (3, 1, 0), (1, 0, 0), (1, 1, 0), (4, 1, 0),
    (2, 0, 3), (3, 0, 1), (5, 0, 0), (3, 0, 2), (4, 0, 1), (2, 1, 3), (4, 0, 2), (5, 1, 0),
    (3, 1, 2), (3, 1, 1), (6, 0, 0), (4, 0, 3), (4, 1, 1), (4, 1, 3), (4, 1, 2), (6, 1, 0),
    (5, 0, 1), (5, 0, 2), (5, 0, 3), (5, 1, 3), (5, 1, 2), (5, 1, 1), (7, 1, 0), (6, 0, 2),
    (6, 0, 3), (6, 0, 1), (6, 1, 3), (6, 1, 2), (6, 1, 1), (7, 0, 2), (7, 0, 3), (7, 0, 1),
    (7, 1, 3), (7, 1, 1), (7, 1, 2), (7, 0, 0), (8, 1, 0), (8, 0, 2), (8, 0, 3), (9, 0, 2),
    (8, 0, 1), (8, 1, 3), (9, 1, 0), (8, 1, 2), (8, 1, 1), (9, 0, 1), (10, 0, 3), (8, 0, 0),
    (9, 1, 2), (9, 1, 1), (10, 0, 2), (10, 1, 3), (10, 0, 1), (9, 0, 0), (10, 1, 2), (10, 1, 0),
    (10, 1, 1), (10, 0, 0),
)
NEAR, FAR, XS, SIB, FIRST, SECOND, GATHER, SPREAD, PAIR, XR, ZR, CROSS_IN, CROSS_OUT = range(13)
Z_FIRST = ((0, 1), (1, 1))


def nn(a, b):
    return jnp.dot(a, b, preferred_element_type=F32)


def nt(a, b):
    return lax.dot_general(a, b, (((1,), (1,)), ((), ())), preferred_element_type=F32)


def lanes_to_rows(v):
    return jnp.concatenate(
        [v[:, 128 * j : 128 * (j + 1)] for j in range(v.shape[1] // 128)], axis=0
    )


def sigmoid_2u(v):
    u = 0.7978845608028654 * (v + 0.044715 * (v * v * v))
    return 1.0 / (1.0 + jnp.exp(jnp.minimum(-2.0 * u, 80.0)))


def kernel(
    mask_in_hbm, mask_out_hbm, tok_hbm, grad_hbm, w_in_hbm, w_out_hbm, out,
    mask_in, mask_out, tok, grad, w_in, w_out, gath, pack, unp, part_f, part_b, y_in,
    half_f, half_b, z_in, pre_s, hid, sib_out, sib_in, x_out, x_in, mine, piece, cross,
    cross_out, cross_in, zh_out, zh_in,
    load_sem, send, got_near, got_far, got_x, got_sib, got_y, got_z, got_gz, got_gy, got_pair, got_xr,
    got_zr,
):
    r, c = lax.axis_index("row"), lax.axis_index("col")
    zl, y = r // 4, r % 4
    zh, x, k = c // 8, (c // 2) % 4, c % 2

    def at_y(d):
        return {"row": zl * 4 + (y + d) % 4}

    def at_zl(d):
        return {"row": ((zl + d) % 4) * 4 + y}

    def at_x(d):
        return {"col": zh * 8 + ((x + d) % 4) * 2 + k}

    def at_zh(d):
        return {"col": ((zh + d) % 4) * 8 + x * 2 + k}

    def at_cross(d):
        return {"col": zh * 8 + ((x + d) % 4) * 2 + (1 - k)}

    def axes(a, p):
        if (a, p) in Z_FIRST:
            return zl, at_zl, y, at_y
        return y, at_y, zl, at_zl

    sibling = at_cross(0)

    barrier = pltpu.get_barrier_semaphore()
    peers = [at_zh(1), at_zh(3)]
    for d in (2, 1, 3):
        peers += [at_x(d), at_y(d), at_zl(d)]
    peers.append(sibling)
    for peer in peers:
        pl.semaphore_signal(barrier, inc=1, device_id=peer, device_id_type=MESH)

    loads = []
    for src, dst in (
        (tok_hbm, tok),
        (grad_hbm, grad),
        (mask_in_hbm, mask_in),
        (mask_out_hbm, mask_out),
        (w_in_hbm, w_in),
        (w_out_hbm, w_out),
    ):
        loads.append(pltpu.make_async_copy(src, dst, load_sem.at[len(loads)]))
        loads[-1].start()

    def put(src, dst, peer, kind, sem):
        pltpu.make_async_remote_copy(
            src_ref=src, dst_ref=dst, send_sem=send.at[kind], recv_sem=sem,
            device_id=peer, device_id_type=MESH,
        ).start()

    def arrive(ref, sem):
        pltpu.make_async_copy(ref, ref, sem).wait()

    for a, v in ((0, tok), (1, grad)):
        loads[a].wait()
        v = v[...].astype(F32)
        pack[a] = jnp.zeros((64, 128), F32)
        for j in range(6):
            pack[a, pl.ds(j, 10, stride=6), :] = v[:, 128 * j : 128 * (j + 1)]
        gath[a, 0, 0, 0] = pack[a].astype(BF16)
        for p in range(4):
            cross[a, p, pl.ds(56, 8), :] = jnp.zeros((8, 128), F32)
            for e in range(4):
                piece[a, p, e, pl.ds(56, 8), :] = jnp.zeros((8, 128), F32)
    pl.semaphore_wait(barrier, len(peers))

    def spread(a, p):
        for e in (2, 1, 3):
            put(gath.at[a, p, 0, 0], gath.at[a, p, 0, 4 - e], at_x(e), XS, got_x.at[a, p])
            if p == 3:
                dst = gath.at[a, 3, 1, 4 - e]
                put(gath.at[a, 3, 0, 0], dst, at_cross(e), CROSS_IN, got_sib.at[a, 3])
        if p == 3:
            put(gath.at[a, 3, 0, 0], gath.at[a, 3, 1, 0], sibling, CROSS_IN, got_sib.at[a, 3])

    top, low = pl.ds(0, 32), pl.ds(32, 32)

    def relay(a, _):
        far = gath.at[a, 3, 0, 0]
        arrive(gath.at[a, 1, 0, 0, top], got_near.at[a, 0])
        put(gath.at[a, 1, 0, 0, top], far.at[top], at_zh(3), FAR, got_far.at[a])
        arrive(gath.at[a, 2, 0, 0, low], got_near.at[a, 1])
        put(gath.at[a, 2, 0, 0, low], far.at[low], at_zh(1), FAR, got_far.at[a])

    def from_near(a, _):
        arrive(gath.at[a, 1, 0, 0, low], got_near.at[a, 2])
        spread(a, 1)
        arrive(gath.at[a, 2, 0, 0, top], got_near.at[a, 3])
        spread(a, 2)

    def from_far(a, p):
        arrive(gath.at[a, 3, 0, 0], got_far.at[a])
        spread(a, p)

    def to_sibling(a, p):
        arrive(gath.at[a, p, 0, pl.ds(1, 3)], got_x.at[a, p])
        put(gath.at[a, p, 0], gath.at[a, p, 1], sibling, SIB, got_sib.at[a, p])

    for i, halves in ((0, (top, low)), (2, (low, top))):
        for a in (0, 1):
            own = gath.at[a, 0, 0, 0]
            for j, p, half, e in ((i, 1, halves[0], 3), (i + 1, 2, halves[1], 1)):
                put(own.at[half], gath.at[a, p, 0, 0, half], at_zh(e), NEAR, got_near.at[a, j])
    for a in (0, 1):
        spread(a, 0)
    for load in loads[2:]:
        load.wait()
    for w, mask in ((w_in, mask_in), (w_out, mask_out)):
        for i in range(6):
            rows = slice(128 * i, 128 * (i + 1))
            for j in range(6):
                cols = slice(128 * j, 128 * (j + 1))
                keep = mask[i, j].astype(F32)
                w[rows, cols] = (w[rows, cols].astype(F32) * keep).astype(BF16)

    def first_product(a, d):
        if d == 3:
            arrive(gath.at[a, 3, 0, pl.ds(1, 3)], got_x.at[a, 3])
        arrive(gath.at[a, d, 1], got_sib.at[a, d])
        for s in range(8):
            unp[a, pl.ds(60 * s, 60), :] = gath[a, d, s // 4, s % 4].astype(F32)[:60]
        left = jnp.concatenate(
            [unp[a, pl.ds(j, 80, stride=6), :].astype(BF16) for j in range(6)], axis=1
        ).astype(BF16)
        value = nn(left, w_in[...]) if a == 0 else nt(left, w_out[...])
        rows = jnp.concatenate([lanes_to_rows(value), jnp.zeros((32, 128), F32)], axis=0)
        for g in range(4):
            part = rows[128 * g : 128 * (g + 1)]
            part_f[a, d, g] = part
            part_b[a, d, g] = part.astype(BF16)
        i, at, _, _ = axes(a, d)
        for e in (2, 1, 3):
            put(part_b.at[a, d, (i + e) % 4], y_in.at[a, d, 4 - e], at(e), FIRST, got_y.at[a, d])

    def sum_over_y(a, d):
        arrive(y_in.at[a, d, pl.ds(1, 3)], got_y.at[a, d])
        first, _, i, at = axes(a, d)
        total = part_f[a, d, first]
        for e in (1, 2, 3):
            total = total + y_in[a, d, e].astype(F32)
        for q in range(4):
            rows = total[32 * q : 32 * (q + 1)]
            half_f[a, d, q] = rows
            half_b[a, d, q] = rows.astype(BF16)
        for e in (2, 1, 3):
            put(half_b.at[a, d, (i + e) % 4], z_in.at[a, d, 4 - e], at(e), SECOND, got_z.at[a, d])

    def activate(a, d):
        arrive(z_in.at[a, d, pl.ds(1, 3)], got_z.at[a, d])
        i, at_i, j, at_j = axes(a, d)
        total = half_f[a, d, j]
        for e in (1, 2, 3):
            total = total + z_in[a, d, e].astype(F32)
        if a == 0:
            pre_s[d] = total
            value = total * sigmoid_2u(total)
        else:
            v = pre_s[d]
            s = sigmoid_2u(v)
            slope = 1.5957691216057308 * (1.0 + 0.134145 * (v * v))
            value = (s + v * (s * (1.0 - s)) * slope) * total
        hid[a, d, i, j] = value.astype(BF16)
        slot = hid.at[a, d, i, j]
        for e in (1, 2, 3):
            put(slot, slot, at_j(e), GATHER, got_gz.at[a, d, e - 1])
        for e in (1, 3, 2):
            put(slot, slot, at_i(e), SPREAD, got_gy.at[a, d])

    def pass_on(a, d):
        i, at, j, _ = axes(a, d)
        for e in (1, 3, 2):
            slot = hid.at[a, d, i, (j + 4 - e) % 4]
            arrive(slot, got_gz.at[a, d, e - 1])
            for f in (1, 3, 2):
                put(slot, slot, at(f), SPREAD, got_gy.at[a, d])

    def second_product(a, d):
        arrive(hid.at[a, d, pl.ds(0, 3)], got_gy.at[a, d])
        rows = hid[a, d].reshape(512, 128)
        left = jnp.concatenate([rows[80 * j : 80 * (j + 1)] for j in range(6)], axis=1)
        value = nn(left, w_out[...]) if a == 0 else nt(left, w_in[...])
        mine[a, d] = lanes_to_rows(value[:40])
        sib_out[a, d] = lanes_to_rows(value[40:])
        if d < 3:
            put(sib_out.at[a, d], sib_in.at[a, d], sibling, PAIR, got_pair.at[a, d])
        else:
            for e in (2, 1, 3, 0):
                to_x(a, 3, e)
                for j in range(6):
                    rows = sib_out[a, 3, pl.ds(40 * j + 10 * e, 10), :]
                    cross[a, e, pl.ds(10 * j, 10), :] = rows
                cross_out[a, e] = cross[a, e].astype(BF16)
                dst = cross_in.at[a, (4 - e) % 4]
                put(cross_out.at[a, e], dst, at_cross(e), CROSS_OUT, got_pair.at[a, 3])

    def to_x(a, d, e):
        for j in range(6):
            piece[a, d, e, pl.ds(10 * j, 10), :] = mine[a, d, pl.ds(40 * j + 10 * e, 10), :]
        if e:
            x_out[a, d, e] = piece[a, d, e].astype(BF16)
            put(x_out.at[a, d, e], x_in.at[a, d, 4 - e], at_x(e), XR, got_xr.at[a, d])

    def sum_over_cores(a, d):
        arrive(sib_in.at[a, d], got_pair.at[a, d])
        mine[a, d] = mine[a, d] + sib_in[a, d]
        for e in (2, 1, 3, 0):
            to_x(a, d, e)

    def sum_over_x(a, p):
        arrive(x_in.at[a, p, pl.ds(1, 3)], got_xr.at[a, p])
        total = piece[a, p, 0]
        for e in (1, 2, 3):
            total = total + x_in[a, p, e].astype(F32)
        if p == 3:
            arrive(cross_in.at[a], got_pair.at[a, 3])
            for e in range(4):
                total = total + cross_in[a, e].astype(F32)
        e = PLACES[p]
        if e:
            zh_out[a, e] = total.astype(BF16)
            put(zh_out.at[a, e], zh_in.at[a, 4 - e], at_zh(e), ZR, got_zr.at[a])
        else:
            piece[a, 0, 0] = total

    stages = (
        relay, from_near, from_far, to_sibling, first_product, sum_over_y, activate, pass_on,
        second_product, sum_over_cores, sum_over_x,
    )
    for stage, a, p in ORDER:
        stages[stage](a, p)
    for a in (0, 1):
        arrive(zh_in.at[a, pl.ds(1, 3)], got_zr.at[a])
        total = piece[a, 0, 0]
        for e in (1, 2, 3):
            total = total + zh_in[a, e].astype(F32)
        piece[a, 0, 0] = total
        out[a] = jnp.concatenate(
            [piece[a, 0, 0, pl.ds(10 * j, 10), :] for j in range(6)], axis=1
        ).astype(BF16)
    every = slice(None)
    for kind, ref in (
        (NEAR, gath.at[0, 0, 0]),
        (FAR, gath.at[0, 0, 0, pl.ds(0, 2)]),
        (XS, gath.at[every, every, 0, pl.ds(1, 3)]),
        (SIB, gath.at[every, pl.ds(0, 3), 0]),
        (CROSS_IN, gath.at[every, 3, 1]),
        (FIRST, y_in.at[every, every, pl.ds(1, 3)]),
        (SECOND, z_in.at[every, every, pl.ds(1, 3)]),
        (GATHER, z_in.at[every, every, pl.ds(1, 3)]),
        (SPREAD, hid.at[every, every, pl.ds(0, 3)]),
        (PAIR, sib_in),
        (CROSS_OUT, cross_in),
        (XR, x_in.at[every, every, pl.ds(1, 3)]),
        (ZR, zh_in.at[every, pl.ds(1, 3)]),
    ):
        arrive(ref, send.at[kind])


def on_device(tokens, weight_in, weight_out, mask_in, mask_out, grad_out):
    vmem = pl.BlockSpec(memory_space=pltpu.VMEM)
    hbm = pl.BlockSpec(memory_space=pltpu.HBM)
    shape = jax.ShapeDtypeStruct((2,) + tokens.shape, BF16)
    o = pl.pallas_call(
        kernel,
        out_shape=shape,
        in_specs=[hbm] * 6,
        out_specs=vmem,
        scratch_shapes=[
            pltpu.SMEM(mask_in.shape, jnp.int32),
            pltpu.SMEM(mask_out.shape, jnp.int32),
            pltpu.VMEM(tokens.shape, BF16),
            pltpu.VMEM(tokens.shape, BF16),
            pltpu.VMEM((768, 768), BF16),
            pltpu.VMEM((768, 768), BF16),
            pltpu.VMEM((2, 4, 2, 4, 64, 128), BF16),
            pltpu.VMEM((2, 64, 128), F32),
            pltpu.VMEM((2, 480, 128), F32),
            pltpu.VMEM((2, 4, 4, 128, 128), F32),
            pltpu.VMEM((2, 4, 4, 128, 128), BF16),
            pltpu.VMEM((2, 4, 4, 128, 128), BF16),
            pltpu.VMEM((2, 4, 4, 32, 128), F32),
            pltpu.VMEM((2, 4, 4, 32, 128), BF16),
            pltpu.VMEM((2, 4, 4, 32, 128), BF16),
            pltpu.VMEM((4, 32, 128), F32),
            pltpu.VMEM((2, 4, 4, 4, 32, 128), BF16),
            pltpu.VMEM((2, 4, 240, 128), F32),
            pltpu.VMEM((2, 3, 240, 128), F32),
            pltpu.VMEM((2, 4, 4, 64, 128), BF16),
            pltpu.VMEM((2, 4, 4, 64, 128), BF16),
            pltpu.VMEM((2, 4, 240, 128), F32),
            pltpu.VMEM((2, 4, 4, 64, 128), F32),
            pltpu.VMEM((2, 4, 64, 128), F32),
            pltpu.VMEM((2, 4, 64, 128), BF16),
            pltpu.VMEM((2, 4, 64, 128), BF16),
            pltpu.VMEM((2, 4, 64, 128), BF16),
            pltpu.VMEM((2, 4, 64, 128), BF16),
            pltpu.SemaphoreType.DMA((6,)),
            pltpu.SemaphoreType.DMA((13,)),
            pltpu.SemaphoreType.DMA((2, 4)),
            pltpu.SemaphoreType.DMA((2,)),
            pltpu.SemaphoreType.DMA((2, 4)),
            pltpu.SemaphoreType.DMA((2, 4)),
            pltpu.SemaphoreType.DMA((2, 4)),
            pltpu.SemaphoreType.DMA((2, 4)),
            pltpu.SemaphoreType.DMA((2, 4, 3)),
            pltpu.SemaphoreType.DMA((2, 4)),
            pltpu.SemaphoreType.DMA((2, 4)),
            pltpu.SemaphoreType.DMA((2, 4)),
            pltpu.SemaphoreType.DMA((2,)),
        ],
        compiler_params=pltpu.CompilerParams(
            collective_id=0, has_side_effects=True, vmem_limit_bytes=60 * 2**20
        ),
    )(mask_in, mask_out, tokens, grad_out, weight_in, weight_out)
    return o[0], o[1]


def solution(mesh):
    placed = (
        P("col", "row"),
        P("row", "col"),
        P("col", "row"),
        P("row", "col"),
        P("col", "row"),
        P("col", "row"),
    )
    return jax.shard_map(
        on_device,
        mesh=mesh,
        in_specs=placed,
        out_specs=(P("col", "row"), P("col", "row")),
        check_vma=False,
    )
```

```python
import jax
import jax.numpy as jnp
from jax import lax
from jax.experimental import pallas as pl
from jax.experimental.pallas import tpu as pltpu
from jax.sharding import PartitionSpec as P

F32, BF16 = jnp.float32, jnp.bfloat16
MESH = pl.DeviceIdType.MESH
PLACES = (0, 1, 3, 2)
ORDER = (
    (3, 0, 0), (0, 0, 0), (4, 0, 0), (0, 1, 0), (3, 1, 0), (1, 0, 0), (1, 1, 0), (4, 1, 0),
    (2, 0, 3), (3, 0, 1), (5, 0, 0), (3, 0, 2), (4, 0, 1), (2, 1, 3), (4, 0, 2), (5, 1, 0),
    (3, 1, 2), (3, 1, 1), (6, 0, 0), (4, 0, 3), (4, 1, 1), (4, 1, 3), (4, 1, 2), (6, 1, 0),
    (5, 0, 1), (5, 0, 2), (5, 0, 3), (5, 1, 3), (5, 1, 2), (5, 1, 1), (7, 1, 0), (6, 0, 2),
    (6, 0, 3), (6, 0, 1), (6, 1, 3), (6, 1, 2), (6, 1, 1), (7, 0, 2), (7, 0, 3), (7, 0, 1),
    (7, 1, 3), (7, 1, 1), (7, 1, 2), (7, 0, 0), (8, 1, 0), (8, 0, 2), (8, 0, 3), (9, 0, 2),
    (8, 0, 1), (8, 1, 3), (9, 1, 0), (8, 1, 2), (8, 1, 1), (9, 0, 1), (10, 0, 3), (8, 0, 0),
    (9, 1, 2), (9, 1, 1), (10, 0, 2), (10, 1, 3), (10, 0, 1), (9, 0, 0), (10, 1, 2), (10, 1, 0),
    (10, 1, 1), (10, 0, 0),
)
NEAR, FAR, XS, SIB, FIRST, SECOND, GATHER, SPREAD, PAIR, XR, ZR, CROSS_IN, CROSS_OUT = range(13)
Z_FIRST = ((0, 1), (1, 1))


def nn(a, b):
    return jnp.dot(a, b, preferred_element_type=F32)


def nt(a, b):
    return lax.dot_general(a, b, (((1,), (1,)), ((), ())), preferred_element_type=F32)


def lanes_to_rows(v):
    return jnp.concatenate(
        [v[:, 128 * j : 128 * (j + 1)] for j in range(v.shape[1] // 128)], axis=0
    )


def sigmoid_2u(v):
    u = 0.7978845608028654 * (v + 0.044715 * (v * v * v))
    return 1.0 / (1.0 + jnp.exp(jnp.minimum(-2.0 * u, 80.0)))


def kernel(
    mask_in_hbm, mask_out_hbm, tok_hbm, grad_hbm, w_in_hbm, w_out_hbm, out,
    mask_in, mask_out, tok, grad, w_in, w_out, gath, pack, unp, part_f, part_b, y_in,
    half_f, half_b, z_in, pre_s, hid, sib_out, sib_in, x_out, x_in, mine, piece, cross,
    cross_out, cross_in, zh_out, zh_in,
    load_sem, send, got_near, got_far, got_x, got_sib, got_y, got_z, got_gz, got_gy, got_pair, got_xr,
    got_zr,
):
    r, c = lax.axis_index("row"), lax.axis_index("col")
    zl, y = r // 4, r % 4
    zh, x, k = c // 8, (c // 2) % 4, c % 2

    def at_y(d):
        return {"row": zl * 4 + (y + d) % 4}

    def at_zl(d):
        return {"row": ((zl + d) % 4) * 4 + y}

    def at_x(d):
        return {"col": zh * 8 + ((x + d) % 4) * 2 + k}

    def at_zh(d):
        return {"col": ((zh + d) % 4) * 8 + x * 2 + k}

    def at_cross(d):
        return {"col": zh * 8 + ((x + d) % 4) * 2 + (1 - k)}

    def axes(a, p):
        if (a, p) in Z_FIRST:
            return zl, at_zl, y, at_y
        return y, at_y, zl, at_zl

    sibling = at_cross(0)

    barrier = pltpu.get_barrier_semaphore()
    peers = [at_zh(1), at_zh(3)]
    for d in (2, 1, 3):
        peers += [at_x(d), at_y(d), at_zl(d)]
    peers.append(sibling)
    for peer in peers:
        pl.semaphore_signal(barrier, inc=1, device_id=peer, device_id_type=MESH)

    loads = []
    for src, dst in (
        (tok_hbm, tok),
        (grad_hbm, grad),
        (mask_in_hbm, mask_in),
        (mask_out_hbm, mask_out),
        (w_in_hbm, w_in),
        (w_out_hbm, w_out),
    ):
        loads.append(pltpu.make_async_copy(src, dst, load_sem.at[len(loads)]))
        loads[-1].start()

    def put(src, dst, peer, kind, sem):
        pltpu.make_async_remote_copy(
            src_ref=src, dst_ref=dst, send_sem=send.at[kind], recv_sem=sem,
            device_id=peer, device_id_type=MESH,
        ).start()

    def arrive(ref, sem):
        pltpu.make_async_copy(ref, ref, sem).wait()

    for a, v in ((0, tok), (1, grad)):
        loads[a].wait()
        v = v[...].astype(F32)
        pack[a] = jnp.zeros((64, 128), F32)
        for j in range(6):
            pack[a, pl.ds(j, 10, stride=6), :] = v[:, 128 * j : 128 * (j + 1)]
        gath[a, 0, 0, 0] = pack[a].astype(BF16)
        for p in range(4):
            cross[a, p, pl.ds(56, 8), :] = jnp.zeros((8, 128), F32)
            for e in range(4):
                piece[a, p, e, pl.ds(56, 8), :] = jnp.zeros((8, 128), F32)
    pl.semaphore_wait(barrier, len(peers))

    def spread(a, p):
        for e in (2, 1, 3):
            put(gath.at[a, p, 0, 0], gath.at[a, p, 0, 4 - e], at_x(e), XS, got_x.at[a, p])
            if p == 3:
                dst = gath.at[a, 3, 1, 4 - e]
                put(gath.at[a, 3, 0, 0], dst, at_cross(e), CROSS_IN, got_sib.at[a, 3])
        if p == 3:
            put(gath.at[a, 3, 0, 0], gath.at[a, 3, 1, 0], sibling, CROSS_IN, got_sib.at[a, 3])

    top, low = pl.ds(0, 32), pl.ds(32, 32)

    def relay(a, _):
        far = gath.at[a, 3, 0, 0]
        arrive(gath.at[a, 1, 0, 0, top], got_near.at[a, 0])
        put(gath.at[a, 1, 0, 0, top], far.at[top], at_zh(3), FAR, got_far.at[a])
        arrive(gath.at[a, 2, 0, 0, low], got_near.at[a, 1])
        put(gath.at[a, 2, 0, 0, low], far.at[low], at_zh(1), FAR, got_far.at[a])

    def from_near(a, _):
        arrive(gath.at[a, 1, 0, 0, low], got_near.at[a, 2])
        spread(a, 1)
        arrive(gath.at[a, 2, 0, 0, top], got_near.at[a, 3])
        spread(a, 2)

    def from_far(a, p):
        arrive(gath.at[a, 3, 0, 0], got_far.at[a])
        spread(a, p)

    def to_sibling(a, p):
        arrive(gath.at[a, p, 0, pl.ds(1, 3)], got_x.at[a, p])
        put(gath.at[a, p, 0], gath.at[a, p, 1], sibling, SIB, got_sib.at[a, p])

    for i, halves in ((0, (top, low)), (2, (low, top))):
        for a in (0, 1):
            own = gath.at[a, 0, 0, 0]
            for j, p, half, e in ((i, 1, halves[0], 3), (i + 1, 2, halves[1], 1)):
                put(own.at[half], gath.at[a, p, 0, 0, half], at_zh(e), NEAR, got_near.at[a, j])
    for a in (0, 1):
        spread(a, 0)
    for load in loads[2:]:
        load.wait()
    for w, mask in ((w_in, mask_in), (w_out, mask_out)):
        for i in range(6):
            rows = slice(128 * i, 128 * (i + 1))
            for j in range(6):
                cols = slice(128 * j, 128 * (j + 1))
                keep = mask[i, j].astype(F32)
                w[rows, cols] = (w[rows, cols].astype(F32) * keep).astype(BF16)

    def first_product(a, d):
        if d == 3:
            arrive(gath.at[a, 3, 0, pl.ds(1, 3)], got_x.at[a, 3])
        arrive(gath.at[a, d, 1], got_sib.at[a, d])
        for s in range(8):
            unp[a, pl.ds(60 * s, 60), :] = gath[a, d, s // 4, s % 4].astype(F32)[:60]
        left = jnp.concatenate(
            [unp[a, pl.ds(j, 80, stride=6), :].astype(BF16) for j in range(6)], axis=1
        ).astype(BF16)
        value = nn(left, w_in[...]) if a == 0 else nt(left, w_out[...])
        rows = jnp.concatenate([lanes_to_rows(value), jnp.zeros((32, 128), F32)], axis=0)
        for g in range(4):
            part = rows[128 * g : 128 * (g + 1)]
            part_f[a, d, g] = part
            part_b[a, d, g] = part.astype(BF16)
        i, at, _, _ = axes(a, d)
        for e in (2, 1, 3):
            put(part_b.at[a, d, (i + e) % 4], y_in.at[a, d, 4 - e], at(e), FIRST, got_y.at[a, d])

    def sum_over_y(a, d):
        arrive(y_in.at[a, d, pl.ds(1, 3)], got_y.at[a, d])
        first, _, i, at = axes(a, d)
        total = part_f[a, d, first]
        for e in (1, 2, 3):
            total = total + y_in[a, d, e].astype(F32)
        for q in range(4):
            rows = total[32 * q : 32 * (q + 1)]
            half_f[a, d, q] = rows
            half_b[a, d, q] = rows.astype(BF16)
        for e in (2, 1, 3):
            put(half_b.at[a, d, (i + e) % 4], z_in.at[a, d, 4 - e], at(e), SECOND, got_z.at[a, d])

    def activate(a, d):
        arrive(z_in.at[a, d, pl.ds(1, 3)], got_z.at[a, d])
        i, at_i, j, at_j = axes(a, d)
        total = half_f[a, d, j]
        for e in (1, 2, 3):
            total = total + z_in[a, d, e].astype(F32)
        if a == 0:
            pre_s[d] = total
            value = total * sigmoid_2u(total)
        else:
            v = pre_s[d]
            s = sigmoid_2u(v)
            slope = 1.5957691216057308 * (1.0 + 0.134145 * (v * v))
            value = (s + v * (s * (1.0 - s)) * slope) * total
        hid[a, d, i, j] = value.astype(BF16)
        slot = hid.at[a, d, i, j]
        for e in (1, 2, 3):
            put(slot, slot, at_j(e), GATHER, got_gz.at[a, d, e - 1])
        for e in (1, 3, 2):
            put(slot, slot, at_i(e), SPREAD, got_gy.at[a, d])

    def pass_on(a, d):
        i, at, j, _ = axes(a, d)
        for e in (1, 3, 2):
            slot = hid.at[a, d, i, (j + 4 - e) % 4]
            arrive(slot, got_gz.at[a, d, e - 1])
            for f in (1, 3, 2):
                put(slot, slot, at(f), SPREAD, got_gy.at[a, d])

    def second_product(a, d):
        arrive(hid.at[a, d, pl.ds(0, 3)], got_gy.at[a, d])
        rows = hid[a, d].reshape(512, 128)
        left = jnp.concatenate([rows[80 * j : 80 * (j + 1)] for j in range(6)], axis=1)
        value = nn(left, w_out[...]) if a == 0 else nt(left, w_in[...])
        mine[a, d] = lanes_to_rows(value[:40])
        sib_out[a, d] = lanes_to_rows(value[40:])
        if d < 3:
            put(sib_out.at[a, d], sib_in.at[a, d], sibling, PAIR, got_pair.at[a, d])
        else:
            for e in (2, 1, 3, 0):
                to_x(a, 3, e)
                for j in range(6):
                    rows = sib_out[a, 3, pl.ds(40 * j + 10 * e, 10), :]
                    cross[a, e, pl.ds(10 * j, 10), :] = rows
                cross_out[a, e] = cross[a, e].astype(BF16)
                dst = cross_in.at[a, (4 - e) % 4]
                put(cross_out.at[a, e], dst, at_cross(e), CROSS_OUT, got_pair.at[a, 3])

    def to_x(a, d, e):
        for j in range(6):
            piece[a, d, e, pl.ds(10 * j, 10), :] = mine[a, d, pl.ds(40 * j + 10 * e, 10), :]
        if e:
            x_out[a, d, e] = piece[a, d, e].astype(BF16)
            put(x_out.at[a, d, e], x_in.at[a, d, 4 - e], at_x(e), XR, got_xr.at[a, d])

    def sum_over_cores(a, d):
        arrive(sib_in.at[a, d], got_pair.at[a, d])
        mine[a, d] = mine[a, d] + sib_in[a, d]
        for e in (2, 1, 3, 0):
            to_x(a, d, e)

    def sum_over_x(a, p):
        arrive(x_in.at[a, p, pl.ds(1, 3)], got_xr.at[a, p])
        total = piece[a, p, 0]
        for e in (1, 2, 3):
            total = total + x_in[a, p, e].astype(F32)
        if p == 3:
            arrive(cross_in.at[a], got_pair.at[a, 3])
            for e in range(4):
                total = total + cross_in[a, e].astype(F32)
        e = PLACES[p]
        if e:
            zh_out[a, e] = total.astype(BF16)
            put(zh_out.at[a, e], zh_in.at[a, 4 - e], at_zh(e), ZR, got_zr.at[a])
        else:
            piece[a, 0, 0] = total

    stages = (
        relay, from_near, from_far, to_sibling, first_product, sum_over_y, activate, pass_on,
        second_product, sum_over_cores, sum_over_x,
    )
    for stage, a, p in ORDER:
        stages[stage](a, p)
    for a in (0, 1):
        arrive(zh_in.at[a, pl.ds(1, 3)], got_zr.at[a])
        total = piece[a, 0, 0]
        for e in (1, 2, 3):
            total = total + zh_in[a, e].astype(F32)
        piece[a, 0, 0] = total
        out[a] = jnp.concatenate(
            [piece[a, 0, 0, pl.ds(10 * j, 10), :] for j in range(6)], axis=1
        ).astype(BF16)
    every = slice(None)
    for kind, ref in (
        (NEAR, gath.at[0, 0, 0]),
        (FAR, gath.at[0, 0, 0, pl.ds(0, 2)]),
        (XS, gath.at[every, every, 0, pl.ds(1, 3)]),
        (SIB, gath.at[every, pl.ds(0, 3), 0]),
        (CROSS_IN, gath.at[every, 3, 1]),
        (FIRST, y_in.at[every, every, pl.ds(1, 3)]),
        (SECOND, z_in.at[every, every, pl.ds(1, 3)]),
        (GATHER, z_in.at[every, every, pl.ds(1, 3)]),
        (SPREAD, hid.at[every, every, pl.ds(0, 3)]),
        (PAIR, sib_in),
        (CROSS_OUT, cross_in),
        (XR, x_in.at[every, every, pl.ds(1, 3)]),
        (ZR, zh_in.at[every, pl.ds(1, 3)]),
    ):
        arrive(ref, send.at[kind])


def on_device(tokens, weight_in, weight_out, mask_in, mask_out, grad_out):
    vmem = pl.BlockSpec(memory_space=pltpu.VMEM)
    hbm = pl.BlockSpec(memory_space=pltpu.HBM)
    shape = pltpu.VMEM((2,) + tokens.shape, BF16)
    o = pl.pallas_call(
        kernel,
        out_shape=shape,
        in_specs=[hbm] * 6,
        out_specs=vmem,
        scratch_shapes=[
            pltpu.SMEM(mask_in.shape, jnp.int32),
            pltpu.SMEM(mask_out.shape, jnp.int32),
            pltpu.VMEM(tokens.shape, BF16),
            pltpu.VMEM(tokens.shape, BF16),
            pltpu.VMEM((768, 768), BF16),
            pltpu.VMEM((768, 768), BF16),
            pltpu.VMEM((2, 4, 2, 4, 64, 128), BF16),
            pltpu.VMEM((2, 64, 128), F32),
            pltpu.VMEM((2, 480, 128), F32),
            pltpu.VMEM((2, 4, 4, 128, 128), F32),
            pltpu.VMEM((2, 4, 4, 128, 128), BF16),
            pltpu.VMEM((2, 4, 4, 128, 128), BF16),
            pltpu.VMEM((2, 4, 4, 32, 128), F32),
            pltpu.VMEM((2, 4, 4, 32, 128), BF16),
            pltpu.VMEM((2, 4, 4, 32, 128), BF16),
            pltpu.VMEM((4, 32, 128), F32),
            pltpu.VMEM((2, 4, 4, 4, 32, 128), BF16),
            pltpu.VMEM((2, 4, 240, 128), F32),
            pltpu.VMEM((2, 3, 240, 128), F32),
            pltpu.VMEM((2, 4, 4, 64, 128), BF16),
            pltpu.VMEM((2, 4, 4, 64, 128), BF16),
            pltpu.VMEM((2, 4, 240, 128), F32),
            pltpu.VMEM((2, 4, 4, 64, 128), F32),
            pltpu.VMEM((2, 4, 64, 128), F32),
            pltpu.VMEM((2, 4, 64, 128), BF16),
            pltpu.VMEM((2, 4, 64, 128), BF16),
            pltpu.VMEM((2, 4, 64, 128), BF16),
            pltpu.VMEM((2, 4, 64, 128), BF16),
            pltpu.SemaphoreType.DMA((6,)),
            pltpu.SemaphoreType.DMA((13,)),
            pltpu.SemaphoreType.DMA((2, 4)),
            pltpu.SemaphoreType.DMA((2,)),
            pltpu.SemaphoreType.DMA((2, 4)),
            pltpu.SemaphoreType.DMA((2, 4)),
            pltpu.SemaphoreType.DMA((2, 4)),
            pltpu.SemaphoreType.DMA((2, 4)),
            pltpu.SemaphoreType.DMA((2, 4, 3)),
            pltpu.SemaphoreType.DMA((2, 4)),
            pltpu.SemaphoreType.DMA((2, 4)),
            pltpu.SemaphoreType.DMA((2, 4)),
            pltpu.SemaphoreType.DMA((2,)),
        ],
        compiler_params=pltpu.CompilerParams(
            collective_id=0, has_side_effects=True, vmem_limit_bytes=60 * 2**20
        ),
    )(mask_in, mask_out, tokens, grad_out, weight_in, weight_out)
    return o[0], o[1]


def solution(mesh):
    placed = (
        P("col", "row"),
        P("row", "col"),
        P("col", "row"),
        P("row", "col"),
        P("col", "row"),
        P("col", "row"),
    )
    return jax.shard_map(
        on_device,
        mesh=mesh,
        in_specs=placed,
        out_specs=(P("col", "row"), P("col", "row")),
        check_vma=False,
    )
```

```python
import jax
import jax.numpy as jnp
from jax import lax
from jax.experimental import pallas as pl
from jax.experimental.pallas import tpu as pltpu
from jax.sharding import PartitionSpec as P

F32, BF16 = jnp.float32, jnp.bfloat16
MESH = pl.DeviceIdType.MESH
PLACES = (0, 1, 3, 2)
ORDER = (
    (3, 0, 0), (0, 0, 0), (4, 0, 0), (0, 1, 0), (3, 1, 0), (1, 0, 0), (1, 1, 0), (4, 1, 0),
    (2, 0, 3), (3, 0, 1), (5, 0, 0), (3, 0, 2), (4, 0, 1), (2, 1, 3), (4, 0, 2), (5, 1, 0),
    (3, 1, 2), (3, 1, 1), (6, 0, 0), (4, 0, 3), (4, 0, 4), (4, 1, 1), (4, 1, 3), (4, 1, 4),
    (4, 1, 2), (6, 1, 0), (5, 0, 1), (5, 0, 2), (5, 0, 3), (5, 0, 4), (5, 1, 3), (5, 1, 4),
    (5, 1, 2), (5, 1, 1), (6, 0, 2), (6, 0, 3), (6, 0, 4), (6, 0, 1), (6, 1, 3), (7, 1, 0),
    (6, 1, 4), (6, 1, 2), (6, 1, 1), (7, 0, 2), (7, 0, 3), (7, 0, 4), (7, 0, 1), (7, 1, 3),
    (7, 1, 4), (7, 1, 1), (7, 1, 2), (7, 0, 0), (8, 1, 0), (8, 0, 2), (8, 0, 3), (8, 0, 4),
    (9, 0, 2), (8, 0, 1), (8, 1, 3), (8, 1, 4), (9, 1, 0), (8, 1, 2), (8, 1, 1), (9, 0, 1),
    (10, 0, 3), (8, 0, 0), (9, 1, 2), (9, 1, 1), (10, 0, 2), (10, 1, 3), (10, 0, 1), (9, 0, 0),
    (10, 1, 2), (10, 1, 0), (10, 1, 1), (10, 0, 0),
)
NEAR, FAR, XS, SIB, PAIR, XR, ZR, CROSS_IN, CROSS_OUT = range(9)
FIRST, SECOND, GATHER, SPREAD = 9, 11, 13, 15
Z_FIRST = ((0, 1), (1, 1))


def nn(a, b):
    return jnp.dot(a, b, preferred_element_type=F32)


def nt(a, b):
    return lax.dot_general(a, b, (((1,), (1,)), ((), ())), preferred_element_type=F32)


def lanes_to_rows(v):
    return jnp.concatenate(
        [v[:, 128 * j : 128 * (j + 1)] for j in range(v.shape[1] // 128)], axis=0
    )


def sigmoid_2u(v):
    u = 0.7978845608028654 * (v + 0.044715 * (v * v * v))
    return 1.0 / (1.0 + jnp.exp(jnp.minimum(-2.0 * u, 80.0)))


def kernel(
    mask_in_hbm, mask_out_hbm, tok_hbm, grad_hbm, w_in_hbm, w_out_hbm, out,
    mask_in, mask_out, tok, grad, w_in, w_out, gath, pack, unp, part_f, part_b, y_in,
    half_f, half_b, z_in, hid, far_part_f, far_part_b, far_y_in, far_half_f, far_half_b, far_z_in, far_hid, pre_s, sib_out, sib_in, x_out, x_in, mine, piece, cross,
    cross_out, cross_in, zh_out, zh_in,
    send, got_near, got_far, got_x, got_sib, got_y, got_z, got_gz, got_far_gz, got_pair, got_xr,
    got_zr,
):
    r, c = lax.axis_index("row"), lax.axis_index("col")
    zl, y = r // 4, r % 4
    zh, x, k = c // 8, (c // 2) % 4, c % 2

    def at_y(d):
        return {"row": zl * 4 + (y + d) % 4}

    def at_zl(d):
        return {"row": ((zl + d) % 4) * 4 + y}

    def at_x(d):
        return {"col": zh * 8 + ((x + d) % 4) * 2 + k}

    def at_zh(d):
        return {"col": ((zh + d) % 4) * 8 + x * 2 + k}

    def at_cross(d):
        return {"col": zh * 8 + ((x + d) % 4) * 2 + (1 - k)}

    def axes(a, p):
        if (a, p) in Z_FIRST:
            return zl, at_zl, y, at_y
        return y, at_y, zl, at_zl

    sibling = at_cross(0)

    barrier = pltpu.get_barrier_semaphore()
    peers = [at_zh(1), at_zh(3)]
    for d in (2, 1, 3):
        peers += [at_x(d), at_y(d), at_zl(d)]
    peers.append(sibling)
    for peer in peers:
        pl.semaphore_signal(barrier, inc=1, device_id=peer, device_id_type=MESH)

    loads = []
    for src, dst in (
        (tok_hbm, tok),
        (grad_hbm, grad),
        (mask_in_hbm, mask_in),
        (mask_out_hbm, mask_out),
        (w_in_hbm, w_in),
        (w_out_hbm, w_out),
    ):
        loads.append(pltpu.make_async_copy(src, dst, send.at[FIRST + len(loads)]))
        loads[-1].start()

    def put(src, dst, peer, kind, sem):
        pltpu.make_async_remote_copy(
            src_ref=src, dst_ref=dst, send_sem=send.at[kind], recv_sem=sem,
            device_id=peer, device_id_type=MESH,
        ).start()

    def arrive(ref, sem):
        pltpu.make_async_copy(ref, ref, sem).wait()

    for a, v in ((0, tok), (1, grad)):
        loads[a].wait()
        v = v[...].astype(F32)
        pack[a] = jnp.zeros((64, 128), F32)
        for j in range(6):
            pack[a, pl.ds(j, 10, stride=6), :] = v[:, 128 * j : 128 * (j + 1)]
        gath[a, 0, 0, 0] = pack[a].astype(BF16)
        for p in range(4):
            cross[a, p, pl.ds(56, 8), :] = jnp.zeros((8, 128), F32)
            for e in range(4):
                piece[a, p, e, pl.ds(56, 8), :] = jnp.zeros((8, 128), F32)
    pl.semaphore_wait(barrier, len(peers))

    def spread(a, p):
        for e in (2, 1, 3):
            put(gath.at[a, p, 0, 0], gath.at[a, p, 0, 4 - e], at_x(e), XS, got_x.at[a, p])
        if p == 3:
            for e in (2, 1, 3, 0):
                dst = gath.at[a, 3, 1, (4 - e) % 4]
                put(gath.at[a, 3, 0, 0], dst, at_cross(e), CROSS_IN, got_sib.at[a, 3])

    top, low = pl.ds(0, 32), pl.ds(32, 32)

    def relay(a, _):
        far = gath.at[a, 3, 0, 0]
        arrive(gath.at[a, 1, 0, 0], got_near.at[a, 0])
        put(gath.at[a, 1, 0, 0, top], far.at[top], at_zh(3), FAR, got_far.at[a])
        put(gath.at[a, 2, 0, 0, low], far.at[low], at_zh(1), FAR, got_far.at[a])

    def from_near(a, _):
        arrive(gath.at[a, 1, 0, 0], got_near.at[a, 1])
        spread(a, 1)
        spread(a, 2)

    def from_far(a, p):
        arrive(gath.at[a, 3, 0, 0], got_far.at[a])
        spread(a, p)

    def to_sibling(a, p):
        arrive(gath.at[a, p, 0, pl.ds(1, 3)], got_x.at[a, p])
        put(gath.at[a, p, 0], gath.at[a, p, 1], sibling, SIB, got_sib.at[a, p])

    for i, halves in enumerate(((top, low), (low, top))):
        for a in (0, 1):
            own = gath.at[a, 0, 0, 0]
            for p, half, e in ((1, halves[0], 3), (2, halves[1], 1)):
                put(own.at[half], gath.at[a, p, 0, 0, half], at_zh(e), NEAR, got_near.at[a, i])
    for a in (0, 1):
        spread(a, 0)
    for load in loads[2:]:
        load.wait()
    for w, mask in ((w_in, mask_in), (w_out, mask_out)):
        for i in range(6):
            rows = slice(128 * i, 128 * (i + 1))
            for j in range(6):
                cols = slice(128 * j, 128 * (j + 1))
                keep = mask[i, j].astype(F32)
                w[rows, cols] = (w[rows, cols].astype(F32) * keep).astype(BF16)

    near_bank = (part_f, part_b, y_in, half_f, half_b, z_in, hid)
    far_bank = (far_part_f, far_part_b, far_y_in, far_half_f, far_half_b, far_z_in, far_hid)

    def bank(p):
        return (near_bank, p, 80, 128, 0) if p < 3 else (far_bank, p - 3, 40, 64, 1)

    def first_product(a, p):
        (f, b, y_in, *_), u, n, wide, kind = bank(p)
        if p == 3:
            arrive(gath.at[a, 3, 0, pl.ds(1, 3)], got_x.at[a, 3])
            slots = [(3, 0, s) for s in range(4)]
        elif p == 4:
            arrive(gath.at[a, 3, 1], got_sib.at[a, 3])
            slots = [(3, 1, s) for s in range(4)]
        else:
            arrive(gath.at[a, p, 1], got_sib.at[a, p])
            slots = [(p, s // 4, s % 4) for s in range(8)]
        for s, slot in enumerate(slots):
            unp[a, pl.ds(60 * s, 60), :] = gath[(a, *slot)].astype(F32)[:60]
        left = jnp.concatenate(
            [unp[a, pl.ds(j, n, stride=6), :].astype(BF16) for j in range(6)], axis=1
        )
        value = nn(left, w_in[...]) if a == 0 else nt(left, w_out[...])
        fill = jnp.zeros((4 * wide - 6 * n, 128), F32)
        rows = jnp.concatenate([lanes_to_rows(value), fill], axis=0)
        for g in range(4):
            part = rows[wide * g : wide * (g + 1)]
            f[a, u, g] = part
            b[a, u, g] = part.astype(BF16)
        i, at, _, _ = axes(a, p)
        for e in (2, 1, 3):
            put(b.at[a, u, (i + e) % 4], y_in.at[a, u, 4 - e], at(e), FIRST + kind, got_y.at[a, p])

    def sum_over_y(a, p):
        (f, _, y_in, half_f, half_b, z_in, _), u, _, wide, kind = bank(p)
        arrive(y_in.at[a, u, pl.ds(1, 3)], got_y.at[a, p])
        first, _, i, at = axes(a, p)
        total = f[a, u, first]
        for e in (1, 2, 3):
            total = total + y_in[a, u, e].astype(F32)
        for q in range(4):
            rows = total[wide // 4 * q : wide // 4 * (q + 1)]
            half_f[a, u, q] = rows
            half_b[a, u, q] = rows.astype(BF16)
        for e in (2, 1, 3):
            src, dst = half_b.at[a, u, (i + e) % 4], z_in.at[a, u, 4 - e]
            put(src, dst, at(e), SECOND + kind, got_z.at[a, p])

    def gathered(a, p, e):
        if e == 1:
            return got_y.at[a, p]
        if e == 2:
            return got_sib.at[a, p] if p < 3 else got_far_gz.at[a, p - 3]
        return got_gz.at[a, p]

    def spreads(a, p):
        return got_x.at[a, p] if p < 4 else got_sib.at[a, 3]

    def activate(a, p):
        (_, _, _, half_f, _, z_in, hid), u, _, wide, kind = bank(p)
        arrive(z_in.at[a, u, pl.ds(1, 3)], got_z.at[a, p])
        i, at_i, j, at_j = axes(a, p)
        total = half_f[a, u, j]
        for e in (1, 2, 3):
            total = total + z_in[a, u, e].astype(F32)
        if a == 0:
            pre_s[p, pl.ds(0, wide // 4), :] = total
            value = total * sigmoid_2u(total)
        else:
            v = pre_s[p, pl.ds(0, wide // 4), :]
            s = sigmoid_2u(v)
            slope = 1.5957691216057308 * (1.0 + 0.134145 * (v * v))
            value = (s + v * (s * (1.0 - s)) * slope) * total
        hid[a, u, i, j] = value.astype(BF16)
        slot = hid.at[a, u, i, j]
        for e in (1, 2, 3):
            put(slot, slot, at_j(e), GATHER + kind, gathered(a, p, e))
        for e in (1, 3, 2):
            put(slot, slot, at_i(e), SPREAD + kind, spreads(a, p))

    def pass_on(a, p):
        (*_, hid), u, _, _, kind = bank(p)
        i, at, j, _ = axes(a, p)
        for e in (1, 3, 2):
            slot = hid.at[a, u, i, (j + 4 - e) % 4]
            arrive(slot, gathered(a, p, e))
            for f in (1, 3, 2):
                put(slot, slot, at(f), SPREAD + kind, spreads(a, p))

    def second_product(a, p):
        (*_, hid), u, n, wide, _ = bank(p)
        arrive(hid.at[a, u, pl.ds(0, 3)], spreads(a, p))
        rows = hid[a, u].reshape(4 * wide, 128)
        if n % 16:
            rows = rows.astype(F32)
        left = jnp.concatenate([rows[n * j : n * (j + 1)] for j in range(6)], axis=1)
        left = left.astype(BF16)
        value = nn(left, w_out[...]) if a == 0 else nt(left, w_in[...])
        if p < 3:
            mine[a, p] = lanes_to_rows(value[:40])
            sib_out[a, p] = lanes_to_rows(value[40:])
            put(sib_out.at[a, p], sib_in.at[a, p], sibling, PAIR, got_pair.at[a, p])
        elif p == 3:
            mine[a, 3] = lanes_to_rows(value)
            for e in (2, 1, 3, 0):
                to_x(a, 3, e)
        else:
            sib_out[a, 3] = lanes_to_rows(value)
            for e in (2, 1, 3, 0):
                for j in range(6):
                    rows = sib_out[a, 3, pl.ds(40 * j + 10 * e, 10), :]
                    cross[a, e, pl.ds(10 * j, 10), :] = rows
                cross_out[a, e] = cross[a, e].astype(BF16)
                dst = cross_in.at[a, (4 - e) % 4]
                put(cross_out.at[a, e], dst, at_cross(e), CROSS_OUT, got_pair.at[a, 3])

    def to_x(a, d, e):
        for j in range(6):
            piece[a, d, e, pl.ds(10 * j, 10), :] = mine[a, d, pl.ds(40 * j + 10 * e, 10), :]
        if e:
            x_out[a, d, e] = piece[a, d, e].astype(BF16)
            put(x_out.at[a, d, e], x_in.at[a, d, 4 - e], at_x(e), XR, got_xr.at[a, d])

    def sum_over_cores(a, d):
        arrive(sib_in.at[a, d], got_pair.at[a, d])
        mine[a, d] = mine[a, d] + sib_in[a, d]
        for e in (2, 1, 3, 0):
            to_x(a, d, e)

    def sum_over_x(a, p):
        arrive(x_in.at[a, p, pl.ds(1, 3)], got_xr.at[a, p])
        total = piece[a, p, 0]
        for e in (1, 2, 3):
            total = total + x_in[a, p, e].astype(F32)
        if p == 3:
            arrive(cross_in.at[a], got_pair.at[a, 3])
            for e in range(4):
                total = total + cross_in[a, e].astype(F32)
        e = PLACES[p]
        if e:
            zh_out[a, e] = total.astype(BF16)
            put(zh_out.at[a, e], zh_in.at[a, 4 - e], at_zh(e), ZR, got_zr.at[a])
        else:
            piece[a, 0, 0] = total

    stages = (
        relay, from_near, from_far, to_sibling, first_product, sum_over_y, activate, pass_on,
        second_product, sum_over_cores, sum_over_x,
    )
    for stage, a, p in ORDER:
        stages[stage](a, p)
    for a in (0, 1):
        arrive(zh_in.at[a, pl.ds(1, 3)], got_zr.at[a])
        total = piece[a, 0, 0]
        for e in (1, 2, 3):
            total = total + zh_in[a, e].astype(F32)
        piece[a, 0, 0] = total
        out[a] = jnp.concatenate(
            [piece[a, 0, 0, pl.ds(10 * j, 10), :] for j in range(6)], axis=1
        ).astype(BF16)
    every = slice(None)
    for kind, ref in (
        (NEAR, gath.at[0, 0, 0]),
        (FAR, gath.at[0, 0, 0, pl.ds(0, 2)]),
        (XS, gath.at[every, every, 0, pl.ds(1, 3)]),
        (SIB, gath.at[every, pl.ds(0, 3), 0]),
        (CROSS_IN, gath.at[every, 3, 1]),
        (FIRST, y_in.at[every, every, pl.ds(1, 3)]),
        (FIRST + 1, far_y_in.at[every, every, pl.ds(1, 3)]),
        (SECOND, z_in.at[every, every, pl.ds(1, 3)]),
        (SECOND + 1, far_z_in.at[every, every, pl.ds(1, 3)]),
        (GATHER, z_in.at[every, every, pl.ds(1, 3)]),
        (GATHER + 1, far_z_in.at[every, every, pl.ds(1, 3)]),
        (SPREAD, hid.at[every, every, pl.ds(0, 3)]),
        (SPREAD + 1, far_hid.at[every, every, pl.ds(0, 3)]),
        (PAIR, sib_in),
        (CROSS_OUT, cross_in),
        (XR, x_in.at[every, every, pl.ds(1, 3)]),
        (ZR, zh_in.at[every, pl.ds(1, 3)]),
    ):
        arrive(ref, send.at[kind])


def on_device(tokens, weight_in, weight_out, mask_in, mask_out, grad_out):
    vmem = pl.BlockSpec(memory_space=pltpu.VMEM)
    hbm = pl.BlockSpec(memory_space=pltpu.HBM)
    shape = pltpu.VMEM((2,) + tokens.shape, BF16)
    o = pl.pallas_call(
        kernel,
        out_shape=shape,
        in_specs=[hbm] * 6,
        out_specs=vmem,
        scratch_shapes=[
            pltpu.SMEM(mask_in.shape, jnp.int32),
            pltpu.SMEM(mask_out.shape, jnp.int32),
            pltpu.VMEM(tokens.shape, BF16),
            pltpu.VMEM(tokens.shape, BF16),
            pltpu.VMEM((768, 768), BF16),
            pltpu.VMEM((768, 768), BF16),
            pltpu.VMEM((2, 4, 2, 4, 64, 128), BF16),
            pltpu.VMEM((2, 64, 128), F32),
            pltpu.VMEM((2, 480, 128), F32),
            pltpu.VMEM((2, 3, 4, 128, 128), F32),
            pltpu.VMEM((2, 3, 4, 128, 128), BF16),
            pltpu.VMEM((2, 3, 4, 128, 128), BF16),
            pltpu.VMEM((2, 3, 4, 32, 128), F32),
            pltpu.VMEM((2, 3, 4, 32, 128), BF16),
            pltpu.VMEM((2, 3, 4, 32, 128), BF16),
            pltpu.VMEM((2, 3, 4, 4, 32, 128), BF16),
            pltpu.VMEM((2, 2, 4, 64, 128), F32),
            pltpu.VMEM((2, 2, 4, 64, 128), BF16),
            pltpu.VMEM((2, 2, 4, 64, 128), BF16),
            pltpu.VMEM((2, 2, 4, 16, 128), F32),
            pltpu.VMEM((2, 2, 4, 16, 128), BF16),
            pltpu.VMEM((2, 2, 4, 16, 128), BF16),
            pltpu.VMEM((2, 2, 4, 4, 16, 128), BF16),
            pltpu.VMEM((5, 32, 128), F32),
            pltpu.VMEM((2, 4, 240, 128), F32),
            pltpu.VMEM((2, 3, 240, 128), F32),
            pltpu.VMEM((2, 4, 4, 64, 128), BF16),
            pltpu.VMEM((2, 4, 4, 64, 128), BF16),
            pltpu.VMEM((2, 4, 240, 128), F32),
            pltpu.VMEM((2, 4, 4, 64, 128), F32),
            pltpu.VMEM((2, 4, 64, 128), F32),
            pltpu.VMEM((2, 4, 64, 128), BF16),
            pltpu.VMEM((2, 4, 64, 128), BF16),
            pltpu.VMEM((2, 4, 64, 128), BF16),
            pltpu.VMEM((2, 4, 64, 128), BF16),
            pltpu.SemaphoreType.DMA((17,)),
            pltpu.SemaphoreType.DMA((2, 2)),
            pltpu.SemaphoreType.DMA((2,)),
            pltpu.SemaphoreType.DMA((2, 4)),
            pltpu.SemaphoreType.DMA((2, 4)),
            pltpu.SemaphoreType.DMA((2, 5)),
            pltpu.SemaphoreType.DMA((2, 5)),
            pltpu.SemaphoreType.DMA((2, 5)),
            pltpu.SemaphoreType.DMA((2, 2)),
            pltpu.SemaphoreType.DMA((2, 4)),
            pltpu.SemaphoreType.DMA((2, 4)),
            pltpu.SemaphoreType.DMA((2,)),
        ],
        compiler_params=pltpu.CompilerParams(
            collective_id=0, has_side_effects=True, vmem_limit_bytes=60 * 2**20
        ),
    )(mask_in, mask_out, tokens, grad_out, weight_in, weight_out)
    return o[0], o[1]


def solution(mesh):
    placed = (
        P("col", "row"),
        P("row", "col"),
        P("col", "row"),
        P("row", "col"),
        P("col", "row"),
        P("col", "row"),
    )
    return jax.shard_map(
        on_device,
        mesh=mesh,
        in_specs=placed,
        out_specs=(P("col", "row"), P("col", "row")),
        check_vma=False,
    )
```

```python
import jax
import jax.numpy as jnp
from jax import lax
from jax.experimental import pallas as pl
from jax.experimental.pallas import tpu as pltpu
from jax.sharding import PartitionSpec as P

F32, BF16 = jnp.float32, jnp.bfloat16
MESH = pl.DeviceIdType.MESH
PLACES = (0, 1, 3, 2)
ORDER = (
    (3, 0, 0), (0, 0, 0), (4, 0, 0), (0, 1, 0), (3, 1, 0), (1, 0, 0), (1, 1, 0), (4, 1, 0),
    (2, 0, 3), (3, 0, 1), (5, 0, 0), (3, 0, 2), (4, 0, 1), (2, 1, 3), (4, 0, 2), (5, 1, 0),
    (3, 1, 2), (3, 1, 1), (6, 0, 0), (4, 0, 3), (4, 0, 4), (4, 1, 1), (4, 1, 3), (4, 1, 4),
    (4, 1, 2), (6, 1, 0), (5, 0, 1), (5, 0, 2), (5, 0, 3), (5, 0, 4), (5, 1, 3), (5, 1, 4),
    (5, 1, 2), (5, 1, 1), (6, 0, 2), (6, 0, 3), (6, 0, 4), (6, 0, 1), (6, 1, 3), (7, 1, 0),
    (6, 1, 4), (6, 1, 2), (6, 1, 1), (7, 0, 2), (7, 0, 3), (7, 0, 4), (7, 0, 1), (7, 1, 3),
    (7, 1, 4), (7, 1, 1), (7, 1, 2), (7, 0, 0), (8, 1, 0), (8, 0, 2), (8, 0, 3), (8, 0, 4),
    (9, 0, 2), (8, 0, 1), (8, 1, 3), (8, 1, 4), (9, 1, 0), (8, 1, 2), (8, 1, 1), (9, 0, 1),
    (10, 0, 3), (8, 0, 0), (9, 1, 2), (9, 1, 1), (10, 0, 2), (10, 1, 3), (10, 0, 1), (9, 0, 0),
    (10, 1, 2), (10, 1, 0), (10, 1, 1), (10, 0, 0),
)
NEAR, FAR, XS, SIB, PAIR, XR, ZR, CROSS_IN, CROSS_OUT = range(9)
FIRST, SECOND, GATHER, SPREAD = 9, 11, 13, 15
Z_FIRST = ((0, 1), (1, 1))


def nn(a, b):
    return jnp.dot(a, b, preferred_element_type=F32)


def nt(a, b):
    return lax.dot_general(a, b, (((1,), (1,)), ((), ())), preferred_element_type=F32)


def lanes_to_rows(v):
    return jnp.concatenate(
        [v[:, 128 * j : 128 * (j + 1)] for j in range(v.shape[1] // 128)], axis=0
    )


def sigmoid_2u(v):
    u = 0.7978845608028654 * (v + 0.044715 * (v * v * v))
    return 1.0 / (1.0 + jnp.exp(jnp.minimum(-2.0 * u, 80.0)))


def kernel(
    mask_in_hbm, mask_out_hbm, tok_hbm, grad_hbm, w_in_hbm, w_out_hbm, out,
    mask_in, mask_out, tok, grad, w_in, w_out, gath, pack, unp, part_f, part_b, y_in,
    half_f, half_b, z_in, hid, far_part_f, far_part_b, far_y_in, far_half_f, far_half_b, far_z_in, far_hid, pre_s, sib_out, sib_in, x_out, x_in, mine, piece, cross,
    cross_out, cross_in, zh_out, zh_in,
    send, got_near, got_far, got_x, got_sib, got_y, got_z, got_gz, got_far_gz, got_pair, got_xr,
    got_zr,
):
    r, c = lax.axis_index("row"), lax.axis_index("col")
    zl, y = r // 4, r % 4
    zh, x, k = c // 8, (c // 2) % 4, c % 2

    def at_y(d):
        return {"row": zl * 4 + (y + d) % 4}

    def at_zl(d):
        return {"row": ((zl + d) % 4) * 4 + y}

    def at_x(d):
        return {"col": zh * 8 + ((x + d) % 4) * 2 + k}

    def at_zh(d):
        return {"col": ((zh + d) % 4) * 8 + x * 2 + k}

    def at_cross(d):
        return {"col": zh * 8 + ((x + d) % 4) * 2 + (1 - k)}

    def axes(a, p):
        if (a, p) in Z_FIRST:
            return zl, at_zl, y, at_y
        return y, at_y, zl, at_zl

    sibling = at_cross(0)

    barrier = pltpu.get_barrier_semaphore()
    peers = [at_zh(1), at_zh(3)]
    for d in (2, 1, 3):
        peers += [at_x(d), at_y(d), at_zl(d)]
    peers.append(sibling)
    for peer in peers:
        pl.semaphore_signal(barrier, inc=1, device_id=peer, device_id_type=MESH)

    loads = []
    for src, dst in (
        (tok_hbm, tok),
        (grad_hbm, grad),
        (mask_in_hbm, mask_in),
        (mask_out_hbm, mask_out),
        (w_in_hbm, w_in),
        (w_out_hbm, w_out),
    ):
        loads.append(pltpu.make_async_copy(src, dst, send.at[FIRST + len(loads)]))
        loads[-1].start()

    def put(src, dst, peer, kind, sem):
        pltpu.make_async_remote_copy(
            src_ref=src, dst_ref=dst, send_sem=send.at[kind], recv_sem=sem,
            device_id=peer, device_id_type=MESH,
        ).start()

    def arrive(ref, sem):
        pltpu.make_async_copy(ref, ref, sem).wait()

    for a, v in ((0, tok), (1, grad)):
        loads[a].wait()
        v = v[...].astype(F32)
        pack[a] = jnp.zeros((64, 128), F32)
        for j in range(6):
            pack[a, pl.ds(j, 10, stride=6), :] = v[:, 128 * j : 128 * (j + 1)]
        gath[a, 0, 0, 0] = pack[a].astype(BF16)
        for p in range(4):
            cross[a, p, pl.ds(56, 8), :] = jnp.zeros((8, 128), F32)
            for e in range(4):
                piece[a, p, e, pl.ds(56, 8), :] = jnp.zeros((8, 128), F32)
    pl.semaphore_wait(barrier, len(peers))

    def spread(a, p):
        for e in (2, 1, 3):
            put(gath.at[a, p, 0, 0], gath.at[a, p, 0, 4 - e], at_x(e), XS, got_x.at[a, p])
        if p == 3:
            for e in (2, 1, 3, 0):
                dst = gath.at[a, 3, 1, (4 - e) % 4]
                put(gath.at[a, 3, 0, 0], dst, at_cross(e), CROSS_IN, got_sib.at[a, 3])

    top, low = pl.ds(0, 32), pl.ds(32, 32)

    def relay(a, _):
        far = gath.at[a, 3, 0, 0]
        arrive(gath.at[a, 1, 0, 0], got_near.at[a, 0])
        put(gath.at[a, 1, 0, 0, top], far.at[top], at_zh(3), FAR, got_far.at[a])
        put(gath.at[a, 2, 0, 0, low], far.at[low], at_zh(1), FAR, got_far.at[a])

    def from_near(a, _):
        arrive(gath.at[a, 1, 0, 0], got_near.at[a, 1])
        spread(a, 1)
        spread(a, 2)

    def from_far(a, p):
        arrive(gath.at[a, 3, 0, 0], got_far.at[a])
        spread(a, p)

    def to_sibling(a, p):
        arrive(gath.at[a, p, 0, pl.ds(1, 3)], got_x.at[a, p])
        put(gath.at[a, p, 0], gath.at[a, p, 1], sibling, SIB, got_sib.at[a, p])

    for i, halves in enumerate(((top, low), (low, top))):
        for a in (0, 1):
            own = gath.at[a, 0, 0, 0]
            for p, half, e in ((1, halves[0], 3), (2, halves[1], 1)):
                put(own.at[half], gath.at[a, p, 0, 0, half], at_zh(e), NEAR, got_near.at[a, i])
    for a in (0, 1):
        spread(a, 0)
    for load in loads[2:]:
        load.wait()
    for w, mask in ((w_in, mask_in), (w_out, mask_out)):
        for i in range(6):
            rows = slice(128 * i, 128 * (i + 1))
            for j in range(6):
                cols = slice(128 * j, 128 * (j + 1))
                keep = mask[i, j].astype(F32)
                w[rows, cols] = (w[rows, cols].astype(F32) * keep).astype(BF16)

    near_bank = (part_f, part_b, y_in, half_f, half_b, z_in, hid)
    far_bank = (far_part_f, far_part_b, far_y_in, far_half_f, far_half_b, far_z_in, far_hid)

    def bank(p):
        return (near_bank, p, 80, 128, 0) if p < 3 else (far_bank, p - 3, 40, 64, 1)

    def first_product(a, p):
        (f, b, y_in, *_), u, n, wide, kind = bank(p)
        if p == 3:
            arrive(gath.at[a, 3, 0, pl.ds(1, 3)], got_x.at[a, 3])
            slots = [(3, 0, s) for s in range(4)]
        elif p == 4:
            arrive(gath.at[a, 3, 1], got_sib.at[a, 3])
            slots = [(3, 1, s) for s in range(4)]
        else:
            arrive(gath.at[a, p, 1], got_sib.at[a, p])
            slots = [(p, s // 4, s % 4) for s in range(8)]
        for s, slot in enumerate(slots):
            unp[a, pl.ds(60 * s, 60), :] = gath[(a, *slot)].astype(F32)[:60]
        left = jnp.concatenate(
            [unp[a, pl.ds(j, n, stride=6), :].astype(BF16) for j in range(6)], axis=1
        )
        value = nn(left, w_in[...]) if a == 0 else nt(left, w_out[...])
        fill = jnp.zeros((4 * wide - 6 * n, 128), F32)
        rows = jnp.concatenate([lanes_to_rows(value), fill], axis=0)
        for g in range(4):
            part = rows[wide * g : wide * (g + 1)]
            f[a, u, g] = part
            b[a, u, g] = part.astype(BF16)
        i, at, _, _ = axes(a, p)
        for e in (2, 1, 3):
            put(b.at[a, u, (i + e) % 4], y_in.at[a, u, 4 - e], at(e), FIRST + kind, got_y.at[a, p])

    def sum_over_y(a, p):
        (f, _, y_in, half_f, half_b, z_in, _), u, _, wide, kind = bank(p)
        arrive(y_in.at[a, u, pl.ds(1, 3)], got_y.at[a, p])
        first, _, i, at = axes(a, p)
        total = f[a, u, first]
        for e in (1, 2, 3):
            total = total + y_in[a, u, e].astype(F32)
        for q in range(4):
            rows = total[wide // 4 * q : wide // 4 * (q + 1)]
            half_f[a, u, q] = rows
            half_b[a, u, q] = rows.astype(BF16)
        for e in (2, 1, 3):
            src, dst = half_b.at[a, u, (i + e) % 4], z_in.at[a, u, 4 - e]
            put(src, dst, at(e), SECOND + kind, got_z.at[a, p])

    def gathered(a, p, e):
        if e == 1:
            return got_y.at[a, p]
        if e == 2:
            return got_sib.at[a, p] if p < 3 else got_far_gz.at[a, p - 3]
        return got_gz.at[a, p]

    def spreads(a, p):
        return got_x.at[a, p] if p < 4 else got_sib.at[a, 3]

    def activate(a, p):
        (_, _, _, half_f, _, z_in, hid), u, _, wide, kind = bank(p)
        arrive(z_in.at[a, u, pl.ds(1, 3)], got_z.at[a, p])
        i, at_i, j, at_j = axes(a, p)
        total = half_f[a, u, j]
        for e in (1, 2, 3):
            total = total + z_in[a, u, e].astype(F32)
        if a == 0:
            pre_s[p, pl.ds(0, wide // 4), :] = total
            value = total * sigmoid_2u(total)
        else:
            v = pre_s[p, pl.ds(0, wide // 4), :]
            s = sigmoid_2u(v)
            slope = 1.5957691216057308 * (1.0 + 0.134145 * (v * v))
            value = (s + v * (s * (1.0 - s)) * slope) * total
        hid[a, u, i, j] = value.astype(BF16)
        slot = hid.at[a, u, i, j]
        for e in (1, 2, 3):
            put(slot, slot, at_j(e), GATHER + kind, gathered(a, p, e))
        for e in (1, 3, 2):
            put(slot, slot, at_i(e), SPREAD + kind, spreads(a, p))

    def pass_on(a, p):
        (*_, hid), u, _, _, kind = bank(p)
        i, at, j, _ = axes(a, p)
        for e in (1, 3, 2):
            slot = hid.at[a, u, i, (j + 4 - e) % 4]
            arrive(slot, gathered(a, p, e))
            for f in (1, 3, 2):
                put(slot, slot, at(f), SPREAD + kind, spreads(a, p))

    def second_product(a, p):
        (*_, hid), u, n, wide, _ = bank(p)
        arrive(hid.at[a, u, pl.ds(0, 3)], spreads(a, p))
        rows = hid[a, u].reshape(4 * wide, 128)
        if n % 16:
            rows = rows.astype(F32)
        left = jnp.concatenate([rows[n * j : n * (j + 1)] for j in range(6)], axis=1)
        left = left.astype(BF16)
        value = nn(left, w_out[...]) if a == 0 else nt(left, w_in[...])
        if p < 3:
            mine[a, p] = lanes_to_rows(value[:40])
            sib_out[a, p] = lanes_to_rows(value[40:])
            put(sib_out.at[a, p], sib_in.at[a, p], sibling, PAIR, got_pair.at[a, p])
        elif p == 3:
            mine[a, 3] = lanes_to_rows(value)
            for e in (2, 1, 3, 0):
                to_x(a, 3, e)
        else:
            sib_out[a, 3] = lanes_to_rows(value)
            for e in (2, 1, 3, 0):
                for j in range(6):
                    rows = sib_out[a, 3, pl.ds(40 * j + 10 * e, 10), :]
                    cross[a, e, pl.ds(10 * j, 10), :] = rows
                cross_out[a, e] = cross[a, e].astype(BF16)
                dst = cross_in.at[a, (4 - e) % 4]
                put(cross_out.at[a, e], dst, at_cross(e), CROSS_OUT, got_pair.at[a, 3])

    def to_x(a, d, e):
        for j in range(6):
            piece[a, d, e, pl.ds(10 * j, 10), :] = mine[a, d, pl.ds(40 * j + 10 * e, 10), :]
        if e:
            x_out[a, d, e] = piece[a, d, e].astype(BF16)
            put(x_out.at[a, d, e], x_in.at[a, d, 4 - e], at_x(e), XR, got_xr.at[a, d])

    def sum_over_cores(a, d):
        arrive(sib_in.at[a, d], got_pair.at[a, d])
        mine[a, d] = mine[a, d] + sib_in[a, d]
        for e in (2, 1, 3, 0):
            to_x(a, d, e)

    def sum_over_x(a, p):
        arrive(x_in.at[a, p, pl.ds(1, 3)], got_xr.at[a, p])
        total = piece[a, p, 0]
        for e in (1, 2, 3):
            total = total + x_in[a, p, e].astype(F32)
        if p == 3:
            arrive(cross_in.at[a], got_pair.at[a, 3])
            for e in range(4):
                total = total + cross_in[a, e].astype(F32)
        e = PLACES[p]
        if e:
            zh_out[a, e] = total.astype(BF16)
            put(zh_out.at[a, e], zh_in.at[a, 4 - e], at_zh(e), ZR, got_zr.at[a])
        else:
            piece[a, 0, 0] = total

    stages = (
        relay, from_near, from_far, to_sibling, first_product, sum_over_y, activate, pass_on,
        second_product, sum_over_cores, sum_over_x,
    )
    for stage, a, p in ORDER:
        stages[stage](a, p)
    for a in (0, 1):
        arrive(zh_in.at[a, pl.ds(1, 3)], got_zr.at[a])
        total = piece[a, 0, 0]
        for e in (1, 2, 3):
            total = total + zh_in[a, e].astype(F32)
        piece[a, 0, 0] = total
        out[a] = jnp.concatenate(
            [piece[a, 0, 0, pl.ds(10 * j, 10), :] for j in range(6)], axis=1
        ).astype(BF16)
    every = slice(None)
    for kind, ref in (
        (NEAR, gath.at[0, 0, 0]),
        (FAR, gath.at[0, 0, 0, pl.ds(0, 2)]),
        (XS, gath.at[every, every, 0, pl.ds(1, 3)]),
        (SIB, gath.at[every, pl.ds(0, 3), 0]),
        (CROSS_IN, gath.at[every, 3, 1]),
        (FIRST, y_in.at[every, every, pl.ds(1, 3)]),
        (FIRST + 1, far_y_in.at[every, every, pl.ds(1, 3)]),
        (SECOND, z_in.at[every, every, pl.ds(1, 3)]),
        (SECOND + 1, far_z_in.at[every, every, pl.ds(1, 3)]),
        (GATHER, z_in.at[every, every, pl.ds(1, 3)]),
        (GATHER + 1, far_z_in.at[every, every, pl.ds(1, 3)]),
        (SPREAD, hid.at[every, every, pl.ds(0, 3)]),
        (SPREAD + 1, far_hid.at[every, every, pl.ds(0, 3)]),
        (PAIR, sib_in),
        (CROSS_OUT, cross_in),
        (XR, x_in.at[every, every, pl.ds(1, 3)]),
        (ZR, zh_in.at[every, pl.ds(1, 3)]),
    ):
        arrive(ref, send.at[kind])


def on_device(tokens, weight_in, weight_out, mask_in, mask_out, grad_out):
    vmem = pl.BlockSpec(memory_space=pltpu.VMEM)
    hbm = pl.BlockSpec(memory_space=pltpu.HBM)
    shape = pltpu.VMEM((2,) + tokens.shape, BF16)
    o = pl.pallas_call(
        kernel,
        out_shape=shape,
        in_specs=[hbm] * 6,
        out_specs=vmem,
        scratch_shapes=[
            pltpu.SMEM(mask_in.shape, jnp.int32),
            pltpu.SMEM(mask_out.shape, jnp.int32),
            pltpu.VMEM(tokens.shape, BF16),
            pltpu.VMEM(tokens.shape, BF16),
            pltpu.VMEM((768, 768), BF16),
            pltpu.VMEM((768, 768), BF16),
            pltpu.VMEM((2, 4, 2, 4, 64, 128), BF16),
            pltpu.VMEM((4, 64, 128), F32),
            pltpu.VMEM((3, 480, 128), F32),
            pltpu.VMEM((2, 3, 4, 128, 128), F32),
            pltpu.VMEM((2, 3, 4, 128, 128), BF16),
            pltpu.VMEM((2, 3, 4, 128, 128), BF16),
            pltpu.VMEM((2, 3, 4, 32, 128), F32),
            pltpu.VMEM((2, 3, 4, 32, 128), BF16),
            pltpu.VMEM((2, 3, 4, 32, 128), BF16),
            pltpu.VMEM((2, 3, 4, 4, 32, 128), BF16),
            pltpu.VMEM((2, 2, 4, 64, 128), F32),
            pltpu.VMEM((2, 2, 4, 64, 128), BF16),
            pltpu.VMEM((2, 2, 4, 64, 128), BF16),
            pltpu.VMEM((2, 2, 4, 16, 128), F32),
            pltpu.VMEM((2, 2, 4, 16, 128), BF16),
            pltpu.VMEM((2, 2, 4, 16, 128), BF16),
            pltpu.VMEM((2, 2, 4, 4, 16, 128), BF16),
            pltpu.VMEM((5, 32, 128), F32),
            pltpu.VMEM((3, 4, 240, 128), F32),
            pltpu.VMEM((2, 3, 240, 128), F32),
            pltpu.VMEM((2, 4, 4, 64, 128), BF16),
            pltpu.VMEM((2, 4, 4, 64, 128), BF16),
            pltpu.VMEM((3, 4, 240, 128), F32),
            pltpu.VMEM((3, 4, 4, 64, 128), F32),
            pltpu.VMEM((3, 4, 64, 128), F32),
            pltpu.VMEM((2, 4, 64, 128), BF16),
            pltpu.VMEM((2, 4, 64, 128), BF16),
            pltpu.VMEM((2, 4, 64, 128), BF16),
            pltpu.VMEM((2, 4, 64, 128), BF16),
            pltpu.SemaphoreType.DMA((17,)),
            pltpu.SemaphoreType.DMA((2, 2)),
            pltpu.SemaphoreType.DMA((2,)),
            pltpu.SemaphoreType.DMA((2, 4)),
            pltpu.SemaphoreType.DMA((2, 4)),
            pltpu.SemaphoreType.DMA((2, 5)),
            pltpu.SemaphoreType.DMA((2, 5)),
            pltpu.SemaphoreType.DMA((2, 5)),
            pltpu.SemaphoreType.DMA((2, 2)),
            pltpu.SemaphoreType.DMA((2, 4)),
            pltpu.SemaphoreType.DMA((2, 4)),
            pltpu.SemaphoreType.DMA((2,)),
        ],
        compiler_params=pltpu.CompilerParams(
            collective_id=0, has_side_effects=True, vmem_limit_bytes=60 * 2**20
        ),
    )(mask_in, mask_out, tokens, grad_out, weight_in, weight_out)
    return o[0], o[1]


def solution(mesh):
    placed = (
        P("col", "row"),
        P("row", "col"),
        P("col", "row"),
        P("row", "col"),
        P("col", "row"),
        P("col", "row"),
    )
    return jax.shard_map(
        on_device,
        mesh=mesh,
        in_specs=placed,
        out_specs=(P("col", "row"), P("col", "row")),
        check_vma=False,
    )
```

```python
import jax
import jax.numpy as jnp
from jax import lax
from jax.experimental import pallas as pl
from jax.experimental.pallas import tpu as pltpu
from jax.sharding import PartitionSpec as P

F32, BF16 = jnp.float32, jnp.bfloat16
MESH = pl.DeviceIdType.MESH
PLACES = (0, 1, 3, 2)
ORDER = (
    (3, 0, 0), (0, 0, 0), (4, 0, 0), (0, 1, 0), (3, 1, 0), (1, 0, 0), (1, 1, 0), (4, 1, 0),
    (2, 0, 3), (3, 0, 1), (5, 0, 0), (3, 0, 2), (4, 0, 1), (2, 1, 3), (4, 0, 2), (5, 1, 0),
    (3, 1, 2), (3, 1, 1), (6, 0, 0), (4, 0, 3), (4, 0, 4), (4, 1, 1), (4, 1, 3), (4, 1, 4),
    (4, 1, 2), (5, 0, 1), (5, 0, 2), (5, 0, 3), (5, 0, 4), (6, 1, 0), (5, 1, 3), (5, 1, 4),
    (5, 1, 2), (5, 1, 1), (6, 0, 2), (6, 0, 3), (6, 0, 4), (6, 0, 1), (6, 1, 3), (7, 1, 0),
    (6, 1, 4), (6, 1, 2), (6, 1, 1), (7, 0, 2), (7, 0, 3), (7, 0, 4), (7, 0, 1), (7, 1, 3),
    (7, 1, 4), (7, 1, 1), (7, 1, 2), (7, 0, 0), (8, 1, 0), (8, 0, 2), (8, 0, 3), (8, 0, 4),
    (9, 0, 2), (8, 0, 1), (8, 1, 3), (8, 1, 4), (9, 1, 0), (8, 1, 2), (8, 1, 1), (9, 0, 1),
    (10, 0, 3), (8, 0, 0), (9, 1, 2), (9, 1, 1), (10, 0, 2), (10, 1, 3), (10, 0, 1), (9, 0, 0),
    (10, 1, 2), (10, 1, 0), (10, 1, 1), (10, 0, 0),
)
NEAR, FAR, XS, SIB, PAIR, XR, ZR, CROSS_IN, CROSS_OUT = range(9)
FIRST, SECOND, GATHER, SPREAD = 9, 11, 13, 15
Z_FIRST = ((0, 1), (1, 1))


def nn(a, b):
    return jnp.dot(a, b, preferred_element_type=F32)


def nt(a, b):
    return lax.dot_general(a, b, (((1,), (1,)), ((), ())), preferred_element_type=F32)


def lanes_to_rows(v):
    return jnp.concatenate(
        [v[:, 128 * j : 128 * (j + 1)] for j in range(v.shape[1] // 128)], axis=0
    )


def sigmoid_2u(v):
    u = 0.7978845608028654 * (v + 0.044715 * (v * v * v))
    return 1.0 / (1.0 + jnp.exp(jnp.minimum(-2.0 * u, 80.0)))


def kernel(
    mask_in_hbm, mask_out_hbm, tok_hbm, grad_hbm, w_in_hbm, w_out_hbm, out,
    mask_in, mask_out, tok, grad, w_in, w_out, gath, pack, unp, part_f, part_b, y_in,
    half_f, half_b, z_in, hid, far_part_f, far_part_b, far_y_in, far_half_f, far_half_b, far_z_in, far_hid, pre_s, sib_out, sib_in, x_out, x_in, mine, piece, cross,
    cross_out, cross_in, zh_out, zh_in,
    send, got_near, got_far, got_x, got_sib, got_y, got_z, got_gz, got_far_gz, got_pair, got_xr,
    got_zr,
):
    r, c = lax.axis_index("row"), lax.axis_index("col")
    zl, y = r // 4, r % 4
    zh, x, k = c // 8, (c // 2) % 4, c % 2

    def at_y(d):
        return {"row": zl * 4 + (y + d) % 4}

    def at_zl(d):
        return {"row": ((zl + d) % 4) * 4 + y}

    def at_x(d):
        return {"col": zh * 8 + ((x + d) % 4) * 2 + k}

    def at_zh(d):
        return {"col": ((zh + d) % 4) * 8 + x * 2 + k}

    def at_cross(d):
        return {"col": zh * 8 + ((x + d) % 4) * 2 + (1 - k)}

    def axes(a, p):
        if (a, p) in Z_FIRST:
            return zl, at_zl, y, at_y
        return y, at_y, zl, at_zl

    sibling = at_cross(0)

    barrier = pltpu.get_barrier_semaphore()
    peers = [at_zh(1), at_zh(3)]
    for d in (2, 1, 3):
        peers += [at_x(d), at_y(d), at_zl(d)]
    peers.append(sibling)
    for peer in peers:
        pl.semaphore_signal(barrier, inc=1, device_id=peer, device_id_type=MESH)

    loads = []
    for src, dst in (
        (tok_hbm, tok),
        (grad_hbm, grad),
        (mask_in_hbm, mask_in),
        (mask_out_hbm, mask_out),
        (w_in_hbm, w_in),
        (w_out_hbm, w_out),
    ):
        loads.append(pltpu.make_async_copy(src, dst, send.at[FIRST + len(loads)]))
        loads[-1].start()

    def put(src, dst, peer, kind, sem):
        pltpu.make_async_remote_copy(
            src_ref=src, dst_ref=dst, send_sem=send.at[kind], recv_sem=sem,
            device_id=peer, device_id_type=MESH,
        ).start()

    def arrive(ref, sem):
        pltpu.make_async_copy(ref, ref, sem).wait()

    for a, v in ((0, tok), (1, grad)):
        loads[a].wait()
        v = v[...].astype(F32)
        pack[a] = jnp.zeros((64, 128), F32)
        for j in range(6):
            pack[a, pl.ds(j, 10, stride=6), :] = v[:, 128 * j : 128 * (j + 1)]
        gath[a, 0, 0, 0] = pack[a].astype(BF16)
        for p in range(4):
            cross[a, p, pl.ds(56, 8), :] = jnp.zeros((8, 128), F32)
            for e in range(4):
                piece[a, p, e, pl.ds(56, 8), :] = jnp.zeros((8, 128), F32)
    pl.semaphore_wait(barrier, len(peers))

    def spread(a, p):
        for e in (2, 1, 3):
            put(gath.at[a, p, 0, 0], gath.at[a, p, 0, 4 - e], at_x(e), XS, got_x.at[a, p])
        if p == 3:
            for e in (2, 1, 3, 0):
                dst = gath.at[a, 3, 1, (4 - e) % 4]
                put(gath.at[a, 3, 0, 0], dst, at_cross(e), CROSS_IN, got_sib.at[a, 3])

    top, low = pl.ds(0, 32), pl.ds(32, 32)

    def relay(a, _):
        far = gath.at[a, 3, 0, 0]
        arrive(gath.at[a, 1, 0, 0], got_near.at[a, 0])
        put(gath.at[a, 1, 0, 0, top], far.at[top], at_zh(3), FAR, got_far.at[a])
        put(gath.at[a, 2, 0, 0, low], far.at[low], at_zh(1), FAR, got_far.at[a])

    def from_near(a, _):
        arrive(gath.at[a, 1, 0, 0], got_near.at[a, 1])
        spread(a, 1)
        spread(a, 2)

    def from_far(a, p):
        arrive(gath.at[a, 3, 0, 0], got_far.at[a])
        spread(a, p)

    def to_sibling(a, p):
        arrive(gath.at[a, p, 0, pl.ds(1, 3)], got_x.at[a, p])
        put(gath.at[a, p, 0], gath.at[a, p, 1], sibling, SIB, got_sib.at[a, p])

    for i, halves in enumerate(((top, low), (low, top))):
        for a in (0, 1):
            own = gath.at[a, 0, 0, 0]
            for p, half, e in ((1, halves[0], 3), (2, halves[1], 1)):
                put(own.at[half], gath.at[a, p, 0, 0, half], at_zh(e), NEAR, got_near.at[a, i])
    for a in (0, 1):
        spread(a, 0)
    for load in loads[2:]:
        load.wait()
    for w, mask in ((w_in, mask_in), (w_out, mask_out)):
        for i in range(6):
            rows = slice(128 * i, 128 * (i + 1))
            for j in range(6):
                cols = slice(128 * j, 128 * (j + 1))
                keep = mask[i, j].astype(F32)
                w[rows, cols] = (w[rows, cols].astype(F32) * keep).astype(BF16)

    near_bank = (part_f, part_b, y_in, half_f, half_b, z_in, hid)
    far_bank = (far_part_f, far_part_b, far_y_in, far_half_f, far_half_b, far_z_in, far_hid)

    def bank(p):
        return (near_bank, p, 80, 128, 0) if p < 3 else (far_bank, p - 3, 40, 64, 1)

    def first_product(a, p):
        (f, b, y_in, *_), u, n, wide, kind = bank(p)
        if p == 3:
            arrive(gath.at[a, 3, 0, pl.ds(1, 3)], got_x.at[a, 3])
            slots = [(3, 0, s) for s in range(4)]
        elif p == 4:
            arrive(gath.at[a, 3, 1], got_sib.at[a, 3])
            slots = [(3, 1, s) for s in range(4)]
        else:
            arrive(gath.at[a, p, 1], got_sib.at[a, p])
            slots = [(p, s // 4, s % 4) for s in range(8)]
        for s, slot in enumerate(slots):
            unp[a, pl.ds(60 * s, 60), :] = gath[(a, *slot)].astype(F32)[:60]
        left = jnp.concatenate(
            [unp[a, pl.ds(j, n, stride=6), :].astype(BF16) for j in range(6)], axis=1
        )
        value = nn(left, w_in[...]) if a == 0 else nt(left, w_out[...])
        fill = jnp.zeros((4 * wide - 6 * n, 128), F32)
        rows = jnp.concatenate([lanes_to_rows(value), fill], axis=0)
        for g in range(4):
            part = rows[wide * g : wide * (g + 1)]
            f[a, u, g] = part
            b[a, u, g] = part.astype(BF16)
        i, at, _, _ = axes(a, p)
        for e in (2, 1, 3):
            put(b.at[a, u, (i + e) % 4], y_in.at[a, u, 4 - e], at(e), FIRST + kind, got_y.at[a, p])

    def sum_over_y(a, p):
        (f, _, y_in, half_f, half_b, z_in, _), u, _, wide, kind = bank(p)
        arrive(y_in.at[a, u, pl.ds(1, 3)], got_y.at[a, p])
        first, _, i, at = axes(a, p)
        total = f[a, u, first]
        for e in (1, 2, 3):
            total = total + y_in[a, u, e].astype(F32)
        for q in range(4):
            rows = total[wide // 4 * q : wide // 4 * (q + 1)]
            half_f[a, u, q] = rows
            half_b[a, u, q] = rows.astype(BF16)
        for e in (2, 1, 3):
            src, dst = half_b.at[a, u, (i + e) % 4], z_in.at[a, u, 4 - e]
            put(src, dst, at(e), SECOND + kind, got_z.at[a, p])

    def gathered(a, p, e):
        if e == 1:
            return got_y.at[a, p]
        if e == 2:
            return got_sib.at[a, p] if p < 3 else got_far_gz.at[a, p - 3]
        return got_gz.at[a, p]

    def spreads(a, p):
        return got_x.at[a, p] if p < 4 else got_sib.at[a, 3]

    def activate(a, p):
        (_, _, _, half_f, _, z_in, hid), u, _, wide, kind = bank(p)
        arrive(z_in.at[a, u, pl.ds(1, 3)], got_z.at[a, p])
        i, at_i, j, at_j = axes(a, p)
        total = half_f[a, u, j]
        for e in (1, 2, 3):
            total = total + z_in[a, u, e].astype(F32)
        if a == 0:
            pre_s[p, pl.ds(0, wide // 4), :] = total
            value = total * sigmoid_2u(total)
        else:
            v = pre_s[p, pl.ds(0, wide // 4), :]
            s = sigmoid_2u(v)
            slope = 1.5957691216057308 * (1.0 + 0.134145 * (v * v))
            value = (s + v * (s * (1.0 - s)) * slope) * total
        hid[a, u, i, j] = value.astype(BF16)
        slot = hid.at[a, u, i, j]
        for e in (1, 2, 3):
            put(slot, slot, at_j(e), GATHER + kind, gathered(a, p, e))
        for e in (1, 3, 2):
            put(slot, slot, at_i(e), SPREAD + kind, spreads(a, p))

    def pass_on(a, p):
        (*_, hid), u, _, _, kind = bank(p)
        i, at, j, _ = axes(a, p)
        for e in (1, 3, 2):
            slot = hid.at[a, u, i, (j + 4 - e) % 4]
            arrive(slot, gathered(a, p, e))
            for f in (1, 3, 2):
                put(slot, slot, at(f), SPREAD + kind, spreads(a, p))

    def second_product(a, p):
        (*_, hid), u, n, wide, _ = bank(p)
        arrive(hid.at[a, u, pl.ds(0, 3)], spreads(a, p))
        rows = hid[a, u].reshape(4 * wide, 128)
        if n % 16:
            rows = rows.astype(F32)
        left = jnp.concatenate([rows[n * j : n * (j + 1)] for j in range(6)], axis=1)
        left = left.astype(BF16)
        value = nn(left, w_out[...]) if a == 0 else nt(left, w_in[...])
        if p < 3:
            mine[a, p] = lanes_to_rows(value[:40])
            sib_out[a, p] = lanes_to_rows(value[40:])
            put(sib_out.at[a, p], sib_in.at[a, p], sibling, PAIR, got_pair.at[a, p])
        elif p == 3:
            mine[a, 3] = lanes_to_rows(value)
            for e in (2, 1, 3, 0):
                to_x(a, 3, e)
        else:
            sib_out[a, 3] = lanes_to_rows(value)
            for e in (2, 1, 3, 0):
                for j in range(6):
                    rows = sib_out[a, 3, pl.ds(40 * j + 10 * e, 10), :]
                    cross[a, e, pl.ds(10 * j, 10), :] = rows
                cross_out[a, e] = cross[a, e].astype(BF16)
                dst = cross_in.at[a, (4 - e) % 4]
                put(cross_out.at[a, e], dst, at_cross(e), CROSS_OUT, got_pair.at[a, 3])

    def to_x(a, d, e):
        for j in range(6):
            piece[a, d, e, pl.ds(10 * j, 10), :] = mine[a, d, pl.ds(40 * j + 10 * e, 10), :]
        if e:
            x_out[a, d, e] = piece[a, d, e].astype(BF16)
            put(x_out.at[a, d, e], x_in.at[a, d, 4 - e], at_x(e), XR, got_xr.at[a, d])

    def sum_over_cores(a, d):
        arrive(sib_in.at[a, d], got_pair.at[a, d])
        mine[a, d] = mine[a, d] + sib_in[a, d]
        for e in (2, 1, 3, 0):
            to_x(a, d, e)

    def sum_over_x(a, p):
        arrive(x_in.at[a, p, pl.ds(1, 3)], got_xr.at[a, p])
        total = piece[a, p, 0]
        for e in (1, 2, 3):
            total = total + x_in[a, p, e].astype(F32)
        if p == 3:
            arrive(cross_in.at[a], got_pair.at[a, 3])
            for e in range(4):
                total = total + cross_in[a, e].astype(F32)
        e = PLACES[p]
        if e:
            zh_out[a, e] = total.astype(BF16)
            put(zh_out.at[a, e], zh_in.at[a, 4 - e], at_zh(e), ZR, got_zr.at[a])
        else:
            piece[a, 0, 0] = total

    stages = (
        relay, from_near, from_far, to_sibling, first_product, sum_over_y, activate, pass_on,
        second_product, sum_over_cores, sum_over_x,
    )
    for stage, a, p in ORDER:
        stages[stage](a, p)
    for a in (0, 1):
        arrive(zh_in.at[a, pl.ds(1, 3)], got_zr.at[a])
        total = piece[a, 0, 0]
        for e in (1, 2, 3):
            total = total + zh_in[a, e].astype(F32)
        piece[a, 0, 0] = total
        out[a] = jnp.concatenate(
            [piece[a, 0, 0, pl.ds(10 * j, 10), :] for j in range(6)], axis=1
        ).astype(BF16)
    every = slice(None)
    for kind, ref in (
        (NEAR, gath.at[0, 0, 0]),
        (FAR, gath.at[0, 0, 0, pl.ds(0, 2)]),
        (XS, gath.at[every, every, 0, pl.ds(1, 3)]),
        (SIB, gath.at[every, pl.ds(0, 3), 0]),
        (CROSS_IN, gath.at[every, 3, 1]),
        (FIRST, y_in.at[every, every, pl.ds(1, 3)]),
        (FIRST + 1, far_y_in.at[every, every, pl.ds(1, 3)]),
        (SECOND, z_in.at[every, every, pl.ds(1, 3)]),
        (SECOND + 1, far_z_in.at[every, every, pl.ds(1, 3)]),
        (GATHER, z_in.at[every, every, pl.ds(1, 3)]),
        (GATHER + 1, far_z_in.at[every, every, pl.ds(1, 3)]),
        (SPREAD, hid.at[every, every, pl.ds(0, 3)]),
        (SPREAD + 1, far_hid.at[every, every, pl.ds(0, 3)]),
        (PAIR, sib_in),
        (CROSS_OUT, cross_in),
        (XR, x_in.at[every, every, pl.ds(1, 3)]),
        (ZR, zh_in.at[every, pl.ds(1, 3)]),
    ):
        arrive(ref, send.at[kind])


def on_device(tokens, weight_in, weight_out, mask_in, mask_out, grad_out):
    vmem = pl.BlockSpec(memory_space=pltpu.VMEM)
    hbm = pl.BlockSpec(memory_space=pltpu.HBM)
    shape = pltpu.VMEM((2,) + tokens.shape, BF16)
    o = pl.pallas_call(
        kernel,
        out_shape=shape,
        in_specs=[hbm] * 6,
        out_specs=vmem,
        scratch_shapes=[
            pltpu.SMEM(mask_in.shape, jnp.int32),
            pltpu.SMEM(mask_out.shape, jnp.int32),
            pltpu.VMEM(tokens.shape, BF16),
            pltpu.VMEM(tokens.shape, BF16),
            pltpu.VMEM((768, 768), BF16),
            pltpu.VMEM((768, 768), BF16),
            pltpu.VMEM((2, 4, 2, 4, 64, 128), BF16),
            pltpu.VMEM((4, 64, 128), F32),
            pltpu.VMEM((3, 480, 128), F32),
            pltpu.VMEM((2, 3, 4, 128, 128), F32),
            pltpu.VMEM((2, 3, 4, 128, 128), BF16),
            pltpu.VMEM((2, 3, 4, 128, 128), BF16),
            pltpu.VMEM((2, 3, 4, 32, 128), F32),
            pltpu.VMEM((2, 3, 4, 32, 128), BF16),
            pltpu.VMEM((2, 3, 4, 32, 128), BF16),
            pltpu.VMEM((2, 3, 4, 4, 32, 128), BF16),
            pltpu.VMEM((2, 2, 4, 64, 128), F32),
            pltpu.VMEM((2, 2, 4, 64, 128), BF16),
            pltpu.VMEM((2, 2, 4, 64, 128), BF16),
            pltpu.VMEM((2, 2, 4, 16, 128), F32),
            pltpu.VMEM((2, 2, 4, 16, 128), BF16),
            pltpu.VMEM((2, 2, 4, 16, 128), BF16),
            pltpu.VMEM((2, 2, 4, 4, 16, 128), BF16),
            pltpu.VMEM((5, 32, 128), F32),
            pltpu.VMEM((3, 4, 240, 128), F32),
            pltpu.VMEM((2, 3, 240, 128), F32),
            pltpu.VMEM((2, 4, 4, 64, 128), BF16),
            pltpu.VMEM((2, 4, 4, 64, 128), BF16),
            pltpu.VMEM((3, 4, 240, 128), F32),
            pltpu.VMEM((3, 4, 4, 64, 128), F32),
            pltpu.VMEM((3, 4, 64, 128), F32),
            pltpu.VMEM((2, 4, 64, 128), BF16),
            pltpu.VMEM((2, 4, 64, 128), BF16),
            pltpu.VMEM((2, 4, 64, 128), BF16),
            pltpu.VMEM((2, 4, 64, 128), BF16),
            pltpu.SemaphoreType.DMA((17,)),
            pltpu.SemaphoreType.DMA((2, 2)),
            pltpu.SemaphoreType.DMA((2,)),
            pltpu.SemaphoreType.DMA((2, 4)),
            pltpu.SemaphoreType.DMA((2, 4)),
            pltpu.SemaphoreType.DMA((2, 5)),
            pltpu.SemaphoreType.DMA((2, 5)),
            pltpu.SemaphoreType.DMA((2, 5)),
            pltpu.SemaphoreType.DMA((2, 2)),
            pltpu.SemaphoreType.DMA((2, 4)),
            pltpu.SemaphoreType.DMA((2, 4)),
            pltpu.SemaphoreType.DMA((2,)),
        ],
        compiler_params=pltpu.CompilerParams(
            collective_id=0, has_side_effects=True, vmem_limit_bytes=60 * 2**20
        ),
    )(mask_in, mask_out, tokens, grad_out, weight_in, weight_out)
    return o[0], o[1]


def solution(mesh):
    placed = (
        P("col", "row"),
        P("row", "col"),
        P("col", "row"),
        P("row", "col"),
        P("col", "row"),
        P("col", "row"),
    )
    return jax.shard_map(
        on_device,
        mesh=mesh,
        in_specs=placed,
        out_specs=(P("col", "row"), P("col", "row")),
        check_vma=False,
    )
```
